256 devices in a mesh: tok: 4 (over z_lo), ffn: 8 (over y, z_hi), wid: 8 (over x, core).
Axes of the slice: x: 4, y: 4, z: 8 (z_hi: 2, z_lo: 4; z = z_hi * 4 + z_lo), core: 2. Of those that a mesh axis runs over, the one named last changes fastest.
Arguments:
- grad_out: bfloat16 [4096, 8192], P(('tok', 'ffn'), 'wid'), may hold values from -6 to 6
- hidden: bfloat16 [4096, 14336], P(('tok', 'wid'), 'ffn'), may hold values from -0.09375 to 0.09375
- down_weight: bfloat16 [14336, 8192], P('ffn', 'wid'), may hold values from -0.046875 to 0.046875
Outputs:
- input_grad: bfloat16 [4096, 14336], P(('tok', 'wid'), 'ffn')
- weight_grad: float32 [4, 14336, 8, 256], P('tok', 'ffn', 'wid')
The draws below stay inside these ranges and needn't reach their ends.
All inputs are finite; a program needn't handle non-finite values.
Results may differ from the reference program's by a relative error of at most 0.001.
Values may be sent and summed in bfloat16 or wider, within the bound.
A program may use at most 128 MiB of HBM per device.

```python
import jax
import jax.numpy as jnp

D = 8192
FF = 14336
TOKENS = 4096
COL_GROUPS = 8
COL_PARTS = 4
COLS = 256


def levels(key, dims, cuts, smallest, high):
    def one(dim, shards_of):
        steps = jax.random.uniform(jax.random.fold_in(jax.random.fold_in(key, 6), dim), (shards_of,), jnp.float32, smallest / len(cuts), high / len(cuts))
        return jnp.repeat(jnp.exp(steps), dims[dim] // shards_of).reshape((-1,) + (1,) * (len(dims) - dim - 1))

    gain = one(*cuts[0])
    for cut in cuts[1:]:
        gain = gain * one(*cut)
    return gain


def centred(stream_key, dims, deviation, limit, split=(), dtype=jnp.bfloat16):
    array = jax.random.normal(stream_key, dims, jnp.float32) * deviation
    if len(split) > 0:
        array = levels(stream_key, dims, split, -0.22, 0.18) * array
    return jnp.clip(array, min=-limit, max=limit).astype(dtype)


def setup_inputs(seed: int = 0) -> dict:
    splits = jax.random.split(jax.random.key(seed), 4)
    grad_out = centred(splits[0], (TOKENS, D), 1.0, 6.0, ((0, 32), (1, 8)))
    hidden = centred(splits[1], (TOKENS, FF), TOKENS ** -0.5, 0.09375, ((0, 32), (1, 8)))
    down_weight = centred(splits[2], (FF, D), FF ** -0.5, 0.046875, ((0, 8), (1, 8)))
    return dict(grad_out=grad_out, hidden=hidden, down_weight=down_weight)


def reference(grad_out, hidden, down_weight):
    input_grad = jnp.dot(grad_out, down_weight.T, preferred_element_type=jnp.float32).astype(jnp.bfloat16)
    grouped = grad_out.astype(jnp.float32).reshape(TOKENS, COL_GROUPS, COL_PARTS, COLS)
    weight_grad = jnp.einsum("ti,tbac->aibc", hidden.astype(jnp.float32), grouped)
    return input_grad, weight_grad
```

```python
import functools

import jax
import jax.numpy as jnp
from jax import lax
from jax.experimental import pallas as pl
from jax.experimental.pallas import tpu as pltpu
from jax.sharding import PartitionSpec as P

F32, BF16 = jnp.float32, jnp.bfloat16
MESH = pl.DeviceIdType.MESH
COLS = 256
ROWS = 128
PAD = 16
ORDER = (3, 2, 0, 1)


def encode(dst, value):
    top = jnp.max(jnp.abs(value), axis=0, keepdims=True)
    scale = (1.0 / jnp.maximum(top, 1e-30)).astype(BF16)
    wide = scale.astype(F32)
    step = 64
    for b in range(0, value.shape[0], step):
        u = value[b : b + step] * wide
        u2 = u * u
        dst[b : b + step, :] = (u * jnp.abs(u) * u2 * (u2 * u2)).astype(BF16)
    dst[value.shape[0] :, :] = jnp.broadcast_to(wide, (PAD, value.shape[1])).astype(BF16)


def decode(src, b, step):
    n = src.shape[0] - PAD
    back = 1.0 / src[n:, :].astype(F32)[0:1]
    y = src[b : b + step, :].astype(F32)
    r = lax.rsqrt(jnp.maximum(jnp.abs(y), 1.2e-38))
    r = lax.rsqrt(r)
    r = r * lax.rsqrt(r) * back
    return jnp.where(y == 0.0, 0.0, jnp.where(y < 0.0, -r, r))


def kernel(
    g_in, h_in, w_in, ig_out, wg_out,
    G, GS, H, HT, HU, W, WS, igp, igF, igB, igA, igo, wgs, wgr, wgo,
    gA, gBC, gZ4, gZ, gS, hA, hBC, hS, hZ, wS, iF, iB, iA, q, lW, lG, lH, lO, lP,
    sG, sGS, sH, sHS, sW, sI, sWG,
):
    n_m = H.shape[0]
    t, f, w = lax.axis_index("tok"), lax.axis_index("ffn"), lax.axis_index("wid")
    y, zh, x, c = f // 2, f % 2, w // 2, w % 2
    d = 1 - 2 * c
    half = t // 2
    mid = (t == 1) | (t == 2)
    end = jnp.logical_not(mid)
    xp, xs = lax.rem(x + d + 4, 4), lax.rem(x - d + 4, 4)
    yp, ys = lax.rem(y + d + 4, 4), lax.rem(y - d + 4, 4)
    x2 = lax.rem(x + 2, 4)
    to_xp, to_xs, to_sib = {"wid": xp * 2 + c}, {"wid": xs * 2 + c}, {"wid": x * 2 + 1 - c}
    to_yp, to_ys, to_z4 = {"ffn": yp * 2 + zh}, {"ffn": ys * 2 + zh}, {"ffn": y * 2 + 1 - zh}
    to_zp, to_zq = {"tok": t + 1 - 2 * (t % 2)}, {"tok": 3 - t}

    def send(src, dst, ssem, rsem, dev):
        pltpu.make_async_remote_copy(
            src_ref=src, dst_ref=dst, send_sem=ssem, recv_sem=rsem, device_id=dev, device_id_type=MESH
        ).start()

    def local(src, dst, sem):
        pltpu.make_async_copy(src, dst, sem).start()

    def wait(ref, sem):
        pltpu.make_async_copy(ref, ref, sem).wait()

    def cols(i):
        return pl.ds(pl.multiple_of(i * COLS, COLS), COLS)

    def rows(i, n=ROWS):
        return pl.ds(pl.multiple_of(i * n, n), n)

    def in_cols(j):
        base = jnp.where(j < 2, 3 - j, j - 2)
        return cols(base + half * (3 - 2 * base))

    def gblk(tr, z, yy, j):
        return G.at[rows(tr * 8 + z * 4 + yy), cols(j)]

    def hblk(m, tr, xx):
        return H.at[m, rows(tr * 8 + c * 4 + xx)]

    def zsel(s):
        return zh if s == 0 else 1 - zh

    barrier = pltpu.get_barrier_semaphore()
    for dev in (to_xp, to_xs, to_sib, to_yp, to_ys, to_z4, to_zp):
        pl.semaphore_signal(barrier, inc=1, device_id=dev, device_id_type=MESH)

    @pl.when(mid)
    def _():
        pl.semaphore_signal(barrier, inc=1, device_id=to_zq, device_id_type=MESH)
        pl.semaphore_wait(barrier, 8)

    @pl.when(end)
    def _():
        pl.semaphore_wait(barrier, 7)

    def own_y(j):
        send(g_in.at[:, in_cols(j)], gblk(0, zh, y, j), sG, gA.at[0, 0, j], to_yp)
        send(g_in.at[:, in_cols(j)], gblk(0, zh, y, j), sG, gBC.at[0, 0, j], to_ys)

    def own_x(m):
        send(h_in.at[:, cols(m)], hblk(m, 0, x), sH, hA.at[0, m], to_xp)
        send(h_in.at[:, cols(m)], hblk(m, 0, x), sH, hBC.at[0, m], to_xs)

    def own_z(m):
        send(h_in.at[:, cols(m)], hblk(m, 1, x), sH, hZ.at[m], to_zp)

    for j in range(4):
        send(g_in.at[:, in_cols(j)], gblk(0, zh, y, j), sG, gZ4.at[j], to_z4)
        if j != 2:

            @pl.when(end)
            def _():
                send(g_in.at[:, in_cols(j)], gblk(1, zh, y, j), sG, gZ.at[0, j], to_zp)

        if j == 0:
            own_x(0)

            @pl.when(end)
            def _():
                own_z(0)

    @pl.when(end)
    def _():
        own_z(1)

    for j in range(4):
        local(g_in.at[:, in_cols(j)], gblk(0, zh, y, j), lG)
    for m in range(n_m):
        local(h_in.at[:, cols(m)], hblk(m, 0, x), lH)
    for j in range(4):
        local(w_in.at[:, in_cols(j)], W.at[:, cols(j)], lW)
        send(w_in.at[:, in_cols(j)], WS.at[:, cols(j)], sW, wS, to_sib)
    wait(G.at[0:ROWS], lG)
    wait(H.at[:, 0:ROWS], lH)

    blk = G.at[0:ROWS, 0:COLS]
    two = G.at[0 : 2 * ROWS, 0:COLS]

    def spread_y(tr, s, j):
        z = zsel(s)
        send(gblk(tr, z, y, j), gblk(tr, z, y, j), sG, gA.at[tr, s, j], to_yp)
        send(gblk(tr, z, y, j), gblk(tr, z, y, j), sG, gBC.at[tr, s, j], to_ys)

    def pass_y(tr, s, j):
        z = zsel(s)
        wait(blk, gA.at[tr, s, j])
        send(gblk(tr, z, ys, j), gblk(tr, z, ys, j), sG, gBC.at[tr, s, j], to_yp)

    def step(s, _):
        @pl.when(s < n_m - 1)
        def _():
            own_x(s + 1)

        @pl.when(end & (s < n_m - 2))
        def _():
            own_z(s + 2)

        @pl.when(s < 4)
        def _():
            own_y(s)

            @pl.when(mid & (s != 2))
            def _():
                wait(blk, gZ.at[0, s])
                spread_y(1, 0, s)

        @pl.when(mid & (s < n_m))
        def _():
            wait(blk, hZ.at[s])
            send(hblk(s, 1, x), hblk(s, 1, x), sH, hA.at[1, s], to_xp)
            send(hblk(s, 1, x), hblk(s, 1, x), sH, hBC.at[1, s], to_xs)

        @pl.when(s < n_m)
        def _():
            wait(blk, hA.at[0, s])
            send(hblk(s, 0, xs), hblk(s, 0, xs), sH, hBC.at[0, s], to_xp)

        @pl.when(s < 4)
        def _():
            wait(blk, gZ4.at[s])
            spread_y(0, 1, s)

            @pl.when(end & (s != 2))
            def _():
                send(gblk(0, 1 - zh, y, s), gblk(1, 1 - zh, y, s), sG, gZ.at[1, s], to_zp)

            pass_y(0, 0, s)

        @pl.when((s >= 1) & (s < 5))
        def _():
            j = s - 1

            @pl.when(mid & (j != 2))
            def _():
                wait(blk, gZ.at[1, j])
                spread_y(1, 1, j)
                pass_y(1, 0, j)

            pass_y(0, 1, j)

        @pl.when((s >= 1) & (s < n_m + 1))
        def _():
            m = s - 1

            @pl.when(mid)
            def _():
                wait(blk, hA.at[1, m])
                send(hblk(m, 1, xs), hblk(m, 1, xs), sH, hBC.at[1, m], to_xp)

            wait(two, hBC.at[0, m])
            own = H.at[m, rows(c, 4 * ROWS)]
            send(own, own, sHS, hS.at[0, m], to_sib)

        @pl.when((s >= 2) & (s < n_m + 2) & mid)
        def _():
            m = s - 2
            wait(two, hBC.at[1, m])
            own = H.at[m, rows(2 + c, 4 * ROWS)]
            send(own, own, sHS, hS.at[1, m], to_sib)

        @pl.when((s >= 2) & (s < 6))
        def _():
            j = s - 2

            @pl.when(mid & (j != 2))
            def _():
                pass_y(1, 1, j)

        @pl.when((s >= 3) & (s < 7))
        def _():
            j = s - 3
            wait(two, gBC.at[0, 0, j])
            wait(two, gBC.at[0, 1, j])

            @pl.when(mid & (j != 2))
            def _():
                wait(two, gBC.at[1, 0, j])
                wait(two, gBC.at[1, 1, j])

            send(G.at[rows(1 - c, 4 * ROWS), cols(j)], GS.at[:, cols(j)], sGS, gS, to_sib)

        @pl.when((s >= 3) & (s < n_m + 3))
        def _():
            m = s - 3
            wait(H.at[0, 0 : 4 * ROWS], hS.at[0, m])

            @pl.when(mid)
            def _():
                wait(H.at[0, 0 : 4 * ROWS], hS.at[1, m])
                HT[m % 2] = H[m].T
                encode(wgs.at[0, m], jnp.dot(HT[m % 2], G[:, 0:COLS], preferred_element_type=F32))
                send(wgs.at[0, m], wgr.at[0, m], sWG, q.at[0, m], to_zq)

        @pl.when(mid & (s >= 4) & (s < n_m + 4))
        def _():
            m = s - 4
            encode(wgs.at[1, m], jnp.dot(HT[m % 2], G[:, COLS : 2 * COLS], preferred_element_type=F32))
            send(wgs.at[1, m], wgr.at[1, m], sWG, q.at[1, m], to_zq)

        @pl.when(s == n_m)
        def _():
            wait(W, lW)
            wait(WS, wS)
            wait(GS, gS)

        @pl.when((s >= n_m) & (s < 2 * n_m))
        def _():
            i = s - n_m
            nt = (((1,), (1,)), ((), ()))
            part = lax.dot_general(G[rows(c, 4 * ROWS), :], W[cols(i), :], nt, preferred_element_type=F32)
            part += lax.dot_general(GS[...], WS[cols(i), :], nt, preferred_element_type=F32)
            igp[i] = part.reshape(4, ROWS, COLS)
            send(igp.at[i, x2], igF.at[i], sI, iF.at[i], to_xp)
            send(igp.at[i, xs], igB.at[i], sI, iB.at[i], to_xs)

        @pl.when((s >= n_m + 1) & (s < 2 * n_m + 1))
        def _():
            i = s - n_m - 1
            wait(igF.at[i], iF.at[i])
            igp[i, xp] = igp[i, xp] + igF[i]
            send(igp.at[i, xp], igA.at[i], sI, iA.at[i], to_xp)

        @pl.when(s >= n_m + 2)
        def _():
            i = s - n_m - 2
            wait(igB.at[i], iB.at[i])
            wait(igA.at[i], iA.at[i])
            igo[i] = (igp[i, x] + igB[i] + igA[i]).astype(BF16)
            local(igo.at[i], ig_out.at[:, cols(i)], lO)

        @pl.when(mid & (s >= n_m) & (s < 2 * n_m))
        def _():
            u = s - n_m
            HU[...] = H[u].T
            part = jnp.dot(HU[:, 0 : 8 * ROWS], G[0 : 8 * ROWS, 2 * COLS : 3 * COLS], preferred_element_type=F32)
            wait(wgr.at[0, u], q.at[0, u])
            encode(wgs.at[2, u], part + decode(wgr.at[0, u], 0, COLS))
            send(wgs.at[2, u], wgr.at[2, u], sWG, q.at[2, u], to_zp)
            part = jnp.dot(HU[...], G[:, 3 * COLS :], preferred_element_type=F32)
            wait(wgr.at[1, u], q.at[1, u])
            wgo[u] = part + decode(wgr.at[1, u], 0, COLS)
            local(wgo.at[u], wg_out.at[cols(u)], lP)

        @pl.when(end & (s >= n_m + 1) & (s < 2 * n_m + 1))
        def _():
            u = s - n_m - 1
            HU[:, 0 : 8 * ROWS] = H[u, 0 : 8 * ROWS].T
            part = jnp.dot(HU[:, 0 : 8 * ROWS], G[0 : 8 * ROWS, 2 * COLS : 3 * COLS], preferred_element_type=F32)
            wait(wgr.at[2, u], q.at[2, u])
            wgo[u] = part + decode(wgr.at[2, u], 0, COLS)
            local(wgo.at[u], wg_out.at[cols(u)], lP)

        return 0

    lax.fori_loop(0, 2 * n_m + 2, step, 0)

    @pl.when(mid)
    def _():
        wait(G.at[0 : 46 * ROWS // 4], sG)
        wait(H.at[:, 0 : 6 * ROWS], sH)
        wait(H.at[:, 0 : 8 * ROWS], sHS)
        wait(wgs, sWG)

    @pl.when(end)
    def _():
        wait(G.at[0 : 34 * ROWS // 4], sG)
        wait(H.at[:, 0 : 4 * ROWS], sH)
        wait(H.at[:, 0 : 4 * ROWS], sHS)

    wait(GS, sGS)
    wait(W, sW)
    wait(igp.at[:, 0:3], sI)
    wait(igo, lO)
    wait(wgo, lP)


def shards(grad_out, hidden, down_weight):
    n_m = hidden.shape[1] // COLS
    dma = pltpu.SemaphoreType.DMA
    vm = pltpu.VMEM
    coded = (3, n_m, COLS + PAD, COLS)
    ig, wg = pl.pallas_call(
        kernel,
        out_shape=(
            jax.ShapeDtypeStruct((ROWS, n_m * COLS), BF16),
            jax.ShapeDtypeStruct((n_m * COLS, COLS), F32),
        ),
        in_specs=[pl.BlockSpec(memory_space=pl.ANY)] * 3,
        out_specs=(pl.BlockSpec(memory_space=pl.ANY),) * 2,
        scratch_shapes=[
            vm((16 * ROWS, 4 * COLS), BF16),
            vm((4 * ROWS, 4 * COLS), BF16),
            vm((n_m, 16 * ROWS, COLS), BF16),
            vm((2, COLS, 16 * ROWS), BF16),
            vm((COLS, 16 * ROWS), BF16),
            vm((n_m * COLS, 4 * COLS), BF16),
            vm((n_m * COLS, 4 * COLS), BF16),
            vm((n_m, 4, ROWS, COLS), F32),
            vm((n_m, ROWS, COLS), F32),
            vm((n_m, ROWS, COLS), F32),
            vm((n_m, ROWS, COLS), F32),
            vm((n_m, ROWS, COLS), BF16),
            vm(coded, BF16),
            vm(coded, BF16),
            vm((n_m, COLS, COLS), F32),
            dma((2, 2, 4)), dma((2, 2, 4)), dma((4,)), dma((2, 4)), dma,
            dma((2, n_m)), dma((2, n_m)), dma((2, n_m)), dma((n_m,)), dma,
            dma((n_m,)), dma((n_m,)), dma((n_m,)), dma((3, n_m)),
            dma, dma, dma, dma, dma,
            dma, dma, dma, dma, dma, dma, dma,
        ],
        compiler_params=pltpu.CompilerParams(
            collective_id=0, has_side_effects=True, vmem_limit_bytes=60 * 2**20
        ),
        cost_estimate=pl.CostEstimate(flops=12 * 10**9, bytes_accessed=10**7, transcendentals=0),
    )(grad_out, hidden, down_weight)
    return ig, wg[None, :, None, :]


def solution(mesh):
    placed = (P(("tok", "ffn"), "wid"), P(("tok", "wid"), "ffn"), P("ffn", "wid"))
    return jax.shard_map(
        shards,
        mesh=mesh,
        in_specs=placed,
        out_specs=(P(("tok", "wid"), "ffn"), P("tok", "ffn", "wid", None)),
        check_vma=False,
    )
```

```python
import functools

import jax
import jax.numpy as jnp
from jax import lax
from jax.experimental import pallas as pl
from jax.experimental.pallas import tpu as pltpu
from jax.sharding import PartitionSpec as P

F32, BF16 = jnp.float32, jnp.bfloat16
MESH = pl.DeviceIdType.MESH
COLS = 256
ROWS = 128
PAD = 16
SPAN = 240.0
ARRIVE = (-3, 0, 2, 3)
STRAIGHT = (0, 1)
LAG = 3
FIRST = 6


def encode(dst, value):
    n = value.shape[0]
    top = jnp.max(jnp.abs(value), axis=0, keepdims=True)
    scale = (1.0 / jnp.maximum(top, 1e-30)).astype(BF16).astype(F32)
    for b in range(0, n, 64):
        u = value[b : b + 64] * scale
        y = jnp.exp2(jnp.abs(u) * SPAN - SPAN / 2)
        dst[b : b + 64, :] = jnp.where(u < 0.0, -y, y).astype(BF16)
    dst[n:, :] = jnp.broadcast_to(scale, (PAD, value.shape[1])).astype(BF16)


def decode(src):
    n = src.shape[0] - PAD
    scale = src[n:, :].astype(F32)[0:1]
    y = src[0:n, :].astype(F32)
    u = (jnp.log2(jnp.abs(y)) + SPAN / 2) * (1.0 / (SPAN * scale))
    return jnp.where(y < 0.0, -u, u)


def kernel(
    g_in, h_in, w_in, ig_out, wg_out,
    G, GS, H, HT, W, WS, igp, igs, igr, igo, wgs, wgr, wgo,
    gA, gBC, gZ4, gZ, gS, hA, hBC, hS, hZ, wS, iR, q, lW, lG, lH, lO, lP,
    sG, sGS, sH, sHS, sW, sI, sWG,
):
    n_m = H.shape[0]
    t, f, w = lax.axis_index("tok"), lax.axis_index("ffn"), lax.axis_index("wid")
    y, zh, x, c = f // 2, f % 2, w // 2, w % 2
    d = 1 - 2 * c
    half = t // 2
    mid = (t == 1) | (t == 2)
    end = jnp.logical_not(mid)
    xp, xs = lax.rem(x + d + 4, 4), lax.rem(x - d + 4, 4)
    yp, ys = lax.rem(y + d + 4, 4), lax.rem(y - d + 4, 4)
    x2, y2 = lax.rem(x + 2, 4), lax.rem(y + 2, 4)
    to_xp, to_xs, to_sib = {"wid": xp * 2 + c}, {"wid": xs * 2 + c}, {"wid": x * 2 + 1 - c}
    to_x2, to_y2 = {"wid": x2 * 2 + c}, {"ffn": y2 * 2 + zh}
    to_yp, to_ys, to_z4 = {"ffn": yp * 2 + zh}, {"ffn": ys * 2 + zh}, {"ffn": y * 2 + 1 - zh}
    near = t + 1 - 2 * (t % 2)
    to_zp, to_zq, to_zd = {"tok": near}, {"tok": 3 - t}, {"tok": near, "ffn": y * 2 + 1 - zh}

    def send(src, dst, ssem, rsem, dev):
        pltpu.make_async_remote_copy(
            src_ref=src, dst_ref=dst, send_sem=ssem, recv_sem=rsem, device_id=dev, device_id_type=MESH
        ).start()

    def local(src, dst, sem):
        pltpu.make_async_copy(src, dst, sem).start()

    def wait(ref, sem):
        pltpu.make_async_copy(ref, ref, sem).wait()

    def cols(i):
        return pl.ds(pl.multiple_of(i * COLS, COLS), COLS)

    def rows(i, n=ROWS):
        return pl.ds(pl.multiple_of(i * n, n), n)

    def in_cols(j):
        base = jnp.where(j < 2, 3 - j, j - 2)
        return cols(base + half * (3 - 2 * base))

    def gblk(tr, z, yy, j):
        return G.at[rows(tr * 8 + z * 4 + yy), cols(j)]

    def hblk(m, tr, xx):
        return H.at[m, rows(tr * 8 + c * 4 + xx)]

    def zsel(s):
        return zh if s == 0 else 1 - zh

    def to_ring_y(src, tr, s, j):
        dst = gblk(tr, zsel(s), y, j)
        if j in STRAIGHT:
            for dev in (to_yp, to_ys, to_y2):
                send(src, dst, sG, gBC.at[tr, s, j], dev)
        else:
            send(src, dst, sG, gA.at[tr, s, j], to_yp)
            send(src, dst, sG, gBC.at[tr, s, j], to_ys)

    def own_y(j):
        to_ring_y(g_in.at[:, in_cols(j)], 0, 0, j)

    def to_ring_x(src, tr, m):
        dst = hblk(m, tr, x)
        if isinstance(m, int) and m == 0:
            for dev in (to_xp, to_xs, to_x2):
                send(src, dst, sH, hBC.at[tr, m], dev)
        else:
            send(src, dst, sH, hA.at[tr, m], to_xp)
            send(src, dst, sH, hBC.at[tr, m], to_xs)

    def own_x(m):
        to_ring_x(h_in.at[:, cols(m)], 0, m)

    def own_z(m):
        send(h_in.at[:, cols(m)], hblk(m, 1, x), sH, hZ.at[m], to_zp)

    def own_z4(j):
        send(g_in.at[:, in_cols(j)], gblk(0, zh, y, j), sG, gZ4.at[j], to_z4)

    def own_gz(j):
        send(g_in.at[:, in_cols(j)], gblk(1, zh, y, j), sG, gZ.at[0, j], to_zp)

    for j in range(4):
        local(g_in.at[:, in_cols(j)], gblk(0, zh, y, j), lG)
        local(w_in.at[:, in_cols(j)], W.at[:, cols(j)], lW)
    for m in range(n_m):
        local(h_in.at[:, cols(m)], hblk(m, 0, x), lH)

    barrier = pltpu.get_barrier_semaphore()
    for dev in (to_xp, to_xs, to_x2, to_sib, to_yp, to_ys, to_y2, to_z4, to_zp, to_zd):
        pl.semaphore_signal(barrier, inc=1, device_id=dev, device_id_type=MESH)

    @pl.when(mid)
    def _():
        pl.semaphore_signal(barrier, inc=1, device_id=to_zq, device_id_type=MESH)
        pl.semaphore_wait(barrier, 11)

    @pl.when(end)
    def _():
        pl.semaphore_wait(barrier, 10)

    own_z4(0)
    own_x(0)
    own_y(0)
    own_x(1)
    own_x(2)

    @pl.when(end)
    def _():
        own_gz(0)
        own_z(0)
        send(g_in.at[:, in_cols(0)], gblk(1, zh, y, 0), sG, gZ.at[1, 0], to_zd)

    wait(G.at[0:ROWS], lG)
    wait(H.at[:, 0:ROWS], lH)

    blk = G.at[0:ROWS, 0:COLS]
    two = G.at[0 : 2 * ROWS, 0:COLS]
    three = G.at[0 : 3 * ROWS, 0:COLS]

    def spread_y(tr, s, j):
        to_ring_y(gblk(tr, zsel(s), y, j), tr, s, j)

    def full_y(tr, j):
        for s in range(2):
            wait(three if j in STRAIGHT else two, gBC.at[tr, s, j])

    def pass_y(tr, s, j):
        z = zsel(s)
        wait(blk, gA.at[tr, s, j])
        send(gblk(tr, z, ys, j), gblk(tr, z, ys, j), sG, gBC.at[tr, s, j], to_yp)

    def near_x(m):
        wait(blk, hA.at[0, m])
        send(hblk(m, 0, xs), hblk(m, 0, xs), sH, hBC.at[0, m], to_xp)

    def spread_x(m):
        wait(blk, hZ.at[m])
        to_ring_x(hblk(m, 1, x), 1, m)

    def pass_x(m):
        wait(blk, hA.at[1, m])
        send(hblk(m, 1, xs), hblk(m, 1, xs), sH, hBC.at[1, m], to_xp)

    def share(tr, m):
        wait(three if isinstance(m, int) and m == 0 else two, hBC.at[tr, m])
        own = H.at[m, rows(2 * tr + c, 4 * ROWS)]
        send(own, own, sHS, hS.at[tr, m], to_sib)

    def share_g(j):
        full_y(0, j)
        send(G.at[rows(1 - c, 4 * ROWS), cols(j)], GS.at[:, cols(j)], sGS, gS, to_sib)

    wait(blk, gZ4.at[0])
    spread_y(0, 1, 0)
    own_z4(1)

    @pl.when(end)
    def _():
        own_z(1)
        own_gz(1)

    @pl.when(mid)
    def _():
        wait(blk, gZ.at[0, 0])
        spread_y(1, 0, 0)
        wait(blk, gZ.at[1, 0])
        spread_y(1, 1, 0)
        spread_x(0)

    own_z4(2)
    own_y(1)
    near_x(1)
    own_x(3)
    share(0, 0)
    near_x(2)

    @pl.when(end)
    def _():
        own_z(2)

    @pl.when(mid)
    def _():
        spread_x(1)
        share(1, 0)

    share_g(0)

    def step(s, _):
        def at(k):
            return pl.when(s == k)

        @pl.when(s < n_m - 4)
        def _():
            own_x(s + 4)

        @pl.when(s < n_m - 3)
        def _():
            near_x(s + 3)

        @pl.when(end & (s < n_m - 3))
        def _():
            own_z(s + 3)

        @pl.when(mid & (s < n_m - 2))
        def _():
            spread_x(s + 2)

        @pl.when(s < n_m - 1)
        def _():
            @pl.when(mid)
            def _():
                pass_x(s + 1)

            share(0, s + 1)

        @pl.when(mid & (s >= 1) & (s < n_m))
        def _():
            share(1, s)

        @pl.when(mid & (s == 0))
        def _():
            full_y(1, 0)

        @pl.when(s < n_m)
        def _():
            wait(H.at[0, 0 : 4 * ROWS], hS.at[0, s])

            @pl.when(mid)
            def _():
                wait(H.at[0, 0 : 4 * ROWS], hS.at[1, s])
                HT[s] = H[s].T
                encode(wgs.at[0, s], jnp.dot(HT[s], G[:, 0:COLS], preferred_element_type=F32))
                send(wgs.at[0, s], wgr.at[0, s], sWG, q.at[0, s], to_zq)

        for j, k in ((1, LAG), (3, ARRIVE[3] + 3)):

            @pl.when(mid & (s == k))
            def _():
                full_y(1, j)

        @pl.when(mid & (s >= LAG) & (s < n_m + LAG))
        def _():
            m = s - LAG
            encode(wgs.at[1, m], jnp.dot(HT[m], G[:, COLS : 2 * COLS], preferred_element_type=F32))
            send(wgs.at[1, m], wgr.at[1, m], sWG, q.at[1, m], to_zq)

        for j in (1, 2, 3):
            both = j != 2
            relay = j not in STRAIGHT

            @at(ARRIVE[j] + 2)
            def _():
                if both and relay:

                    @pl.when(mid)
                    def _():
                        pass_y(1, 1, j)

                share_g(j)

            @at(ARRIVE[j] + 1)
            def _():
                if both:

                    @pl.when(mid)
                    def _():
                        wait(blk, gZ.at[1, j])
                        spread_y(1, 1, j)
                        if relay:
                            pass_y(1, 0, j)

                if relay:
                    pass_y(0, 1, j)

            @at(ARRIVE[j])
            def _():
                wait(blk, gZ4.at[j])
                spread_y(0, 1, j)

                if both:

                    @pl.when(end)
                    def _():
                        send(gblk(0, 1 - zh, y, j), gblk(1, 1 - zh, y, j), sG, gZ.at[1, j], to_zp)

                    @pl.when(mid)
                    def _():
                        wait(blk, gZ.at[0, j])
                        spread_y(1, 0, j)

                if relay:
                    pass_y(0, 0, j)

                if j == 1:
                    own_z4(3)
                    own_y(2)

                    @pl.when(end)
                    def _():
                        own_gz(3)

                if j == 2:
                    own_y(3)

        @at(0)
        def _():
            wait(W, lW)

        @pl.when(s < 4)
        def _():
            send(W.at[:, cols(s)], WS.at[:, cols(s)], sW, wS, to_sib)

        @at(FIRST)
        def _():
            wait(WS, wS)
            wait(GS, gS)

        for k in range(2):
            i = 2 * (s - FIRST) + k

            @pl.when((i >= 0) & (i < n_m))
            def _():
                nt = (((1,), (1,)), ((), ()))
                part = lax.dot_general(G[rows(c, 4 * ROWS), :], W[cols(i), :], nt, preferred_element_type=F32)
                part += lax.dot_general(GS[...], WS[cols(i), :], nt, preferred_element_type=F32)
                igp[i] = part.reshape(4, ROWS, COLS)
                encode(igs.at[0, i], igp[i, x2])
                send(igs.at[0, i], igr.at[0, i], sI, iR.at[0, i], to_xp)
                encode(igs.at[1, i], igp[i, xs])
                send(igs.at[1, i], igr.at[1, i], sI, iR.at[1, i], to_xs)

        for k in range(2):
            l = 2 * (s - FIRST - 1) + k

            @pl.when((l >= 0) & (l < n_m))
            def _():
                wait(igr.at[0, l], iR.at[0, l])
                encode(igs.at[2, l], igp[l, xp] + decode(igr.at[0, l]))
                send(igs.at[2, l], igr.at[2, l], sI, iR.at[2, l], to_xp)

        for k in range(2):
            n = 2 * (s - FIRST - 2) + k

            @pl.when((n >= 0) & (n < n_m))
            def _():
                wait(igr.at[1, n], iR.at[1, n])
                wait(igr.at[2, n], iR.at[2, n])
                igo[n] = (igp[n, x] + decode(igr.at[1, n]) + decode(igr.at[2, n])).astype(BF16)
                local(igo.at[n], ig_out.at[:, cols(n)], lO)

        def store(u, value):
            for l in range(2):
                wgo[u, pl.ds(l, COLS, stride=2), :] = value[:, l * ROWS : (l + 1) * ROWS]
            local(wgo.at[u], wg_out.at[rows(u, 2 * COLS)], lP)

        @pl.when(mid & (s >= 4) & (s < n_m + 4))
        def _():
            u = s - 4
            part = jnp.dot(HT[u, :, 0 : 8 * ROWS], G[0 : 8 * ROWS, 2 * COLS : 3 * COLS], preferred_element_type=F32)
            wait(wgr.at[0, u], q.at[0, u])
            encode(wgs.at[2, u], part + decode(wgr.at[0, u]))
            send(wgs.at[2, u], wgr.at[2, u], sWG, q.at[2, u], to_zp)

        @pl.when(mid & (s >= 6) & (s < n_m + 6))
        def _():
            u = s - 6
            part = jnp.dot(HT[u], G[:, 3 * COLS :], preferred_element_type=F32)
            wait(wgr.at[1, u], q.at[1, u])
            store(u, part + decode(wgr.at[1, u]))

        @pl.when(end & (s >= 6) & (s < n_m + 6))
        def _():
            u = s - 6
            part = jnp.dot(H[u, 0 : 8 * ROWS].T, G[0 : 8 * ROWS, 2 * COLS : 3 * COLS], preferred_element_type=F32)
            wait(wgr.at[2, u], q.at[2, u])
            store(u, part + decode(wgr.at[2, u]))

        return 0

    lax.fori_loop(0, n_m + 6, step, 0)

    @pl.when(mid)
    def _():
        wait(G.at[0 : 46 * ROWS // 4], sG)
        wait(H.at[:, 0 : 6 * ROWS], sH)
        wait(H.at[:, 0 : 8 * ROWS], sHS)
        wait(wgs, sWG)

    @pl.when(end)
    def _():
        wait(G.at[0 : 34 * ROWS // 4], sG)
        wait(H.at[:, 0 : 4 * ROWS], sH)
        wait(H.at[:, 0 : 4 * ROWS], sHS)

    wait(GS, sGS)
    wait(W, sW)
    wait(igs, sI)
    wait(igo, lO)
    wait(wgo, lP)


def place(ig, wg, ig_out, wg_out, sems):
    copies = [pltpu.make_async_copy(ig, ig_out, sems.at[0]), pltpu.make_async_copy(wg, wg_out, sems.at[1])]
    for copy in copies:
        copy.start()
    for copy in copies:
        copy.wait()


def shards(grad_out, hidden, down_weight):
    n_m = hidden.shape[1] // COLS
    dma = pltpu.SemaphoreType.DMA
    vm = pltpu.VMEM
    coded = (3, n_m, COLS + PAD, COLS)
    ig, wg = pl.pallas_call(
        kernel,
        out_shape=(
            jax.ShapeDtypeStruct((ROWS, n_m * COLS), BF16),
            jax.ShapeDtypeStruct((n_m * COLS * 2, ROWS), F32),
        ),
        in_specs=[pl.BlockSpec(memory_space=pl.ANY)] * 3,
        out_specs=(pl.BlockSpec(memory_space=pl.ANY),) * 2,
        scratch_shapes=[
            vm((16 * ROWS, 4 * COLS), BF16),
            vm((4 * ROWS, 4 * COLS), BF16),
            vm((n_m, 16 * ROWS, COLS), BF16),
            vm((n_m, COLS, 16 * ROWS), BF16),
            vm((n_m * COLS, 4 * COLS), BF16),
            vm((n_m * COLS, 4 * COLS), BF16),
            vm((n_m, 4, ROWS, COLS), F32),
            vm((3, n_m, ROWS + PAD, COLS), BF16),
            vm((3, n_m, ROWS + PAD, COLS), BF16),
            vm((n_m, ROWS, COLS), BF16),
            vm(coded, BF16),
            vm(coded, BF16),
            vm((n_m, 2 * COLS, ROWS), F32),
            dma((2, 2, 4)), dma((2, 2, 4)), dma((4,)), dma((2, 4)), dma,
            dma((2, n_m)), dma((2, n_m)), dma((2, n_m)), dma((n_m,)), dma,
            dma((3, n_m)), dma((3, n_m)),
            dma, dma, dma, dma, dma,
            dma, dma, dma, dma, dma, dma, dma,
        ],
        compiler_params=pltpu.CompilerParams(
            collective_id=0, has_side_effects=True, vmem_limit_bytes=60 * 2**20
        ),
        cost_estimate=pl.CostEstimate(flops=12 * 10**9, bytes_accessed=10**7, transcendentals=0),
    )(grad_out, hidden, down_weight)
    ig, wg = pl.pallas_call(
        place,
        out_shape=tuple(jax.ShapeDtypeStruct(a.shape, a.dtype) for a in (ig, wg)),
        in_specs=[pl.BlockSpec(memory_space=pltpu.VMEM)] * 2,
        out_specs=(pl.BlockSpec(memory_space=pl.ANY),) * 2,
        scratch_shapes=[dma((2,))],
    )(ig, wg)
    return ig, wg.reshape(1, n_m * COLS, 1, COLS)


def solution(mesh):
    placed = (P(("tok", "ffn"), "wid"), P(("tok", "wid"), "ffn"), P("ffn", "wid"))
    return jax.shard_map(
        shards,
        mesh=mesh,
        in_specs=placed,
        out_specs=(P(("tok", "wid"), "ffn"), P("tok", "ffn", "wid", None)),
        check_vma=False,
    )
```

```python
import functools

import jax
import jax.numpy as jnp
from jax import lax
from jax.experimental import pallas as pl
from jax.experimental.pallas import tpu as pltpu
from jax.sharding import PartitionSpec as P

F32, BF16 = jnp.float32, jnp.bfloat16
MESH = pl.DeviceIdType.MESH
COLS = 256
ROWS = 128
PAD = 16
STEP = 32
SPAN = 240.0
ARRIVE = (-3, 0, 1, 2)
LEAVE = (-3, 2, -1, 3)
NEAR = (-3, 4, -1, 5)
FIRST = 4
LAG = 6
LAST = 8


def encode(dst, value):
    n = value.shape[0]
    top = jnp.max(jnp.abs(value), axis=0, keepdims=True)
    scale = (1.0 / jnp.maximum(top, 1e-30)).astype(BF16).astype(F32)
    for b in blocks(n):
        u = value[b : b + STEP] * scale
        y = jnp.exp2(jnp.abs(u) * SPAN - SPAN / 2)
        dst[b : b + STEP, :] = jnp.where(u < 0.0, -y, y).astype(BF16)
    dst[n:, :] = jnp.broadcast_to(scale, (PAD, value.shape[1])).astype(BF16)


def decode(src, b):
    n = src.shape[0] - PAD
    scale = src[n:, :].astype(F32)[0:1]
    y = src[b : b + STEP, :].astype(F32)
    u = (jnp.log2(jnp.abs(y)) + SPAN / 2) * (1.0 / (SPAN * scale))
    return jnp.where(y < 0.0, -u, u)


def blocks(n):
    return range(0, n, STEP)


def straight(tr, j):
    return True


def kernel(
    g_in, h_in, w_in, ig_out, wg_out,
    G, GS, H, HT, W, WS, igp, igs, igr, igo, sums, wgs, wgr, wgo,
    gA, gBC, gZ4, gZ, gS, hA, hBC, hS, hZ, wS, iR, q, lW, lG, lH, lO, lP,
    sG, sGS, sH, sHS, sW, sI, sWG,
):
    n_m = H.shape[0]
    t, f, w = lax.axis_index("tok"), lax.axis_index("ffn"), lax.axis_index("wid")
    y, zh, x, c = f // 2, f % 2, w // 2, w % 2
    d = 1 - 2 * c
    half = t // 2
    mid = (t == 1) | (t == 2)
    end = jnp.logical_not(mid)
    xp, xs = lax.rem(x + d + 4, 4), lax.rem(x - d + 4, 4)
    yp, ys = lax.rem(y + d + 4, 4), lax.rem(y - d + 4, 4)
    x2, y2 = lax.rem(x + 2, 4), lax.rem(y + 2, 4)
    to_xp, to_xs, to_sib = {"wid": xp * 2 + c}, {"wid": xs * 2 + c}, {"wid": x * 2 + 1 - c}
    to_x2, to_y2 = {"wid": x2 * 2 + c}, {"ffn": y2 * 2 + zh}
    to_yp, to_ys, to_z4 = {"ffn": yp * 2 + zh}, {"ffn": ys * 2 + zh}, {"ffn": y * 2 + 1 - zh}
    near = t + 1 - 2 * (t % 2)
    to_zp, to_zq, to_zd = {"tok": near}, {"tok": 3 - t}, {"tok": near, "ffn": y * 2 + 1 - zh}

    def send(src, dst, ssem, rsem, dev):
        pltpu.make_async_remote_copy(
            src_ref=src, dst_ref=dst, send_sem=ssem, recv_sem=rsem, device_id=dev, device_id_type=MESH
        ).start()

    def local(src, dst, sem):
        pltpu.make_async_copy(src, dst, sem).start()

    def wait(ref, sem):
        pltpu.make_async_copy(ref, ref, sem).wait()

    def cols(i):
        return pl.ds(pl.multiple_of(i * COLS, COLS), COLS)

    def rows(i, n=ROWS):
        return pl.ds(pl.multiple_of(i * n, n), n)

    def in_cols(j):
        base = jnp.where(j < 2, 3 - j, j - 2)
        return cols(base + half * (3 - 2 * base))

    def gblk(tr, z, yy, j):
        return G.at[rows(tr * 8 + z * 4 + yy), cols(j)]

    def hblk(m, tr, xx):
        return H.at[m, rows(tr * 8 + c * 4 + xx)]

    def zsel(s):
        return zh if s == 0 else 1 - zh

    def to_ring_y(src, tr, s, j):
        dst = gblk(tr, zsel(s), y, j)
        if straight(tr, j):
            for dev in (to_yp, to_ys, to_y2):
                send(src, dst, sG, gBC.at[tr, s, j], dev)
        else:
            send(src, dst, sG, gA.at[tr, s, j], to_yp)
            send(src, dst, sG, gBC.at[tr, s, j], to_ys)

    def own_y(j):
        to_ring_y(gblk(0, zh, y, j), 0, 0, j)

    def to_ring_x(src, tr, m):
        dst = hblk(m, tr, x)
        if tr == 1:
            for dev in (to_xp, to_xs, to_x2):
                send(src, dst, sH, hBC.at[tr, m], dev)
        else:
            send(src, dst, sH, hA.at[tr, m], to_xp)
            send(src, dst, sH, hBC.at[tr, m], to_xs)

    def own_x(m):
        to_ring_x(hblk(m, 0, x), 0, m)

    def own_z(m):
        send(hblk(m, 0, x), hblk(m, 1, x), sH, hZ.at[m], to_zp)

    def own_z4(j):
        send(gblk(0, zh, y, j), gblk(0, zh, y, j), sG, gZ4.at[j], to_z4)

    def own_gz(j):
        send(gblk(0, zh, y, j), gblk(1, zh, y, j), sG, gZ.at[0, j], to_zp)

    for j in range(4):
        local(g_in.at[:, in_cols(j)], gblk(0, zh, y, j), lG)
        local(w_in.at[:, in_cols(j)], W.at[:, cols(j)], lW)
    for m in range(n_m):
        local(h_in.at[:, cols(m)], hblk(m, 0, x), lH)

    barrier = pltpu.get_barrier_semaphore()
    for dev in (to_xp, to_xs, to_x2, to_sib, to_yp, to_ys, to_y2, to_z4, to_zp, to_zd):
        pl.semaphore_signal(barrier, inc=1, device_id=dev, device_id_type=MESH)

    @pl.when(mid)
    def _():
        pl.semaphore_signal(barrier, inc=1, device_id=to_zq, device_id_type=MESH)
        pl.semaphore_wait(barrier, 11)

    @pl.when(end)
    def _():
        pl.semaphore_wait(barrier, 10)

    wait(G.at[0:ROWS], lG)
    wait(H.at[:, 0:ROWS], lH)

    @pl.when(end)
    def _():
        own_gz(0)
        own_z(0)
        send(gblk(0, zh, y, 0), gblk(1, zh, y, 0), sG, gZ.at[1, 0], to_zd)
        own_z(1)
        own_z(2)

    own_z4(0)
    own_x(0)
    own_y(0)
    own_x(1)
    own_x(2)

    blk = G.at[0:ROWS, 0:COLS]
    two = G.at[0 : 2 * ROWS, 0:COLS]
    three = G.at[0 : 3 * ROWS, 0:COLS]

    def spread_y(tr, s, j):
        to_ring_y(gblk(tr, zsel(s), y, j), tr, s, j)

    def full_y(tr, j):
        for s in range(2):
            wait(three if straight(tr, j) else two, gBC.at[tr, s, j])

    def pass_y(tr, s, j):
        z = zsel(s)
        wait(blk, gA.at[tr, s, j])
        send(gblk(tr, z, ys, j), gblk(tr, z, ys, j), sG, gBC.at[tr, s, j], to_yp)

    def near_x(m):
        wait(blk, hA.at[0, m])
        send(hblk(m, 0, xs), hblk(m, 0, xs), sH, hBC.at[0, m], to_xp)

    def spread_x(m):
        wait(blk, hZ.at[m])
        to_ring_x(hblk(m, 1, x), 1, m)

    def share(tr, m):
        wait(three if tr == 1 else two, hBC.at[tr, m])
        own = H.at[m, rows(2 * tr + c, 4 * ROWS)]
        send(own, own, sHS, hS.at[tr, m], to_sib)

    def share_g(j):
        full_y(0, j)
        send(G.at[rows(1 - c, 4 * ROWS), cols(j)], GS.at[:, cols(j)], sGS, gS, to_sib)

    near_x(0)

    @pl.when(end)
    def _():
        near_x(1)
        own_z(3)

    wait(blk, gZ4.at[0])
    spread_y(0, 1, 0)

    @pl.when(mid)
    def _():
        near_x(1)
        wait(blk, gZ.at[0, 0])
        spread_y(1, 0, 0)
        wait(blk, gZ.at[1, 0])
        spread_y(1, 1, 0)
        spread_x(0)

    own_z4(1)
    own_z4(2)
    own_z4(3)
    own_y(1)

    @pl.when(end)
    def _():
        own_z(4)

    @pl.when(mid)
    def _():
        spread_x(1)

    near_x(2)
    own_x(3)
    share(0, 0)

    @pl.when(mid)
    def _():
        share(1, 0)

    def step(s, _):
        def at(k):
            return pl.when(s == k)

        @pl.when(s < n_m - 4)
        def _():
            own_x(s + 4)

        @pl.when(s < n_m - 3)
        def _():
            near_x(s + 3)

        @pl.when(end & (s < n_m - 5))
        def _():
            own_z(s + 5)

        @pl.when(mid & (s < n_m - 2))
        def _():
            spread_x(s + 2)

        @pl.when(s < n_m - 1)
        def _():
            share(0, s + 1)

            @pl.when(mid)
            def _():
                share(1, s + 1)

        @at(0)
        def _():
            share_g(0)

            @pl.when(mid)
            def _():
                full_y(1, 0)

        @pl.when(s < n_m)
        def _():
            wait(H.at[0, 0 : 4 * ROWS], hS.at[0, s])

            @pl.when(mid)
            def _():
                wait(H.at[0, 0 : 4 * ROWS], hS.at[1, s])
                HT[s] = H[s].T
                encode(wgs.at[0, s], jnp.dot(HT[s], G[:, 0:COLS], preferred_element_type=F32))
                send(wgs.at[0, s], wgr.at[0, s], sWG, q.at[0, s], to_zq)

        for j, k in ((1, LAG), (3, LAST)):

            @pl.when(mid & (s == k))
            def _():
                full_y(1, j)

        @pl.when(mid & (s >= LAG) & (s < n_m + LAG))
        def _():
            m = s - LAG
            encode(wgs.at[1, m], jnp.dot(HT[m], G[:, COLS : 2 * COLS], preferred_element_type=F32))
            send(wgs.at[1, m], wgr.at[1, m], sWG, q.at[1, m], to_zq)

        for j in (1, 2, 3):

            @at(ARRIVE[j] + 2)
            def _():
                share_g(j)

            @at(ARRIVE[j])
            def _():
                wait(blk, gZ4.at[j])
                spread_y(0, 1, j)

                if j < 3:
                    own_y(j + 1)

        for j in (1, 3):

            @pl.when(end & (s == LEAVE[j]))
            def _():
                own_gz(j)
                send(gblk(0, 1 - zh, y, j), gblk(1, 1 - zh, y, j), sG, gZ.at[1, j], to_zp)

            @pl.when(mid & (s == NEAR[j]))
            def _():
                for k in range(2):
                    wait(blk, gZ.at[k, j])
                    spread_y(1, k, j)

        @at(0)
        def _():
            wait(W, lW)

        @pl.when(s < 4)
        def _():
            send(W.at[:, cols(s)], WS.at[:, cols(s)], sW, wS, to_sib)

        @at(FIRST)
        def _():
            wait(WS, wS)
            wait(GS, gS)

        for k in range(1):
            i = s - FIRST

            @pl.when((i >= 0) & (i < n_m))
            def _():
                nt = (((1,), (1,)), ((), ()))
                part = lax.dot_general(G[rows(c, 4 * ROWS), :], W[cols(i), :], nt, preferred_element_type=F32)
                part += lax.dot_general(GS[...], WS[cols(i), :], nt, preferred_element_type=F32)
                igp[i] = part.reshape(4, ROWS, COLS)
                encode(igs.at[0, i], igp[i, x2])
                send(igs.at[0, i], igr.at[0, i], sI, iR.at[0, i], to_xp)
                encode(igs.at[1, i], igp[i, xs])
                send(igs.at[1, i], igr.at[1, i], sI, iR.at[1, i], to_xs)

        for k in range(1):
            l = s - FIRST - 2

            @pl.when((l >= 0) & (l < n_m))
            def _():
                wait(igr.at[0, l], iR.at[0, l])
                for b in blocks(ROWS):
                    igp[l, xp, b : b + STEP] += decode(igr.at[0, l], b)
                encode(igs.at[2, l], igp[l, xp])
                send(igs.at[2, l], igr.at[2, l], sI, iR.at[2, l], to_xp)

        for k in range(1):
            n = s - FIRST - 4

            @pl.when((n >= 0) & (n < n_m))
            def _():
                wait(igr.at[1, n], iR.at[1, n])
                wait(igr.at[2, n], iR.at[2, n])
                for b in blocks(ROWS):
                    total = igp[n, x, b : b + STEP] + decode(igr.at[1, n], b) + decode(igr.at[2, n], b)
                    igo[n, b : b + STEP] = total.astype(BF16)
                local(igo.at[n], ig_out.at[:, cols(n)], lO)

        def store(u, part, src):
            for b in blocks(COLS):
                value = part[b : b + STEP] + decode(src, b)
                for l in range(2):
                    wgo[u, pl.ds(2 * b + l, STEP, stride=2), :] = value[:, l * ROWS : (l + 1) * ROWS]
            local(wgo.at[u], wg_out.at[rows(u, 2 * COLS)], lP)

        @pl.when(mid & (s >= 4) & (s < n_m + 4))
        def _():
            u = s - 4
            part = jnp.dot(HT[u, :, 0 : 8 * ROWS], G[0 : 8 * ROWS, 2 * COLS : 3 * COLS], preferred_element_type=F32)
            wait(wgr.at[0, u], q.at[0, u])
            for b in blocks(COLS):
                sums[b : b + STEP] = part[b : b + STEP] + decode(wgr.at[0, u], b)
            encode(wgs.at[2, u], sums[...])
            send(wgs.at[2, u], wgr.at[2, u], sWG, q.at[2, u], to_zp)

        @pl.when(mid & (s >= LAST) & (s < n_m + LAST))
        def _():
            u = s - LAST
            part = jnp.dot(HT[u], G[:, 3 * COLS :], preferred_element_type=F32)
            wait(wgr.at[1, u], q.at[1, u])
            store(u, part, wgr.at[1, u])

        @pl.when(end & (s >= 6) & (s < n_m + 6))
        def _():
            u = s - 6
            part = jnp.dot(H[u, 0 : 8 * ROWS].T, G[0 : 8 * ROWS, 2 * COLS : 3 * COLS], preferred_element_type=F32)
            wait(wgr.at[2, u], q.at[2, u])
            store(u, part, wgr.at[2, u])

        return 0

    lax.fori_loop(0, n_m + max(LAST, FIRST + 4), step, 0)

    @pl.when(mid)
    def _():
        wait(G.at[0 : 46 * ROWS // 4], sG)
        wait(H.at[:, 0 : 6 * ROWS], sH)
        wait(H.at[:, 0 : 8 * ROWS], sHS)
        wait(wgs, sWG)

    @pl.when(end)
    def _():
        wait(G.at[0 : 34 * ROWS // 4], sG)
        wait(H.at[:, 0 : 4 * ROWS], sH)
        wait(H.at[:, 0 : 4 * ROWS], sHS)

    wait(GS, sGS)
    wait(W, sW)
    wait(igs, sI)
    wait(igo, lO)
    wait(wgo, lP)


def place(ig, wg, ig_out, wg_out, sems):
    copies = [pltpu.make_async_copy(ig, ig_out, sems.at[0]), pltpu.make_async_copy(wg, wg_out, sems.at[1])]
    for copy in copies:
        copy.start()
    for copy in copies:
        copy.wait()


def shards(grad_out, hidden, down_weight):
    n_m = hidden.shape[1] // COLS
    dma = pltpu.SemaphoreType.DMA
    vm = pltpu.VMEM
    coded = (3, n_m, COLS + PAD, COLS)
    ig, wg = pl.pallas_call(
        kernel,
        out_shape=(
            jax.ShapeDtypeStruct((ROWS, n_m * COLS), BF16),
            jax.ShapeDtypeStruct((n_m * COLS * 2, ROWS), F32),
        ),
        in_specs=[pl.BlockSpec(memory_space=pl.ANY)] * 3,
        out_specs=(pl.BlockSpec(memory_space=pl.ANY),) * 2,
        scratch_shapes=[
            vm((16 * ROWS, 4 * COLS), BF16),
            vm((4 * ROWS, 4 * COLS), BF16),
            vm((n_m, 16 * ROWS, COLS), BF16),
            vm((n_m, COLS, 16 * ROWS), BF16),
            vm((n_m * COLS, 4 * COLS), BF16),
            vm((n_m * COLS, 4 * COLS), BF16),
            vm((n_m, 4, ROWS, COLS), F32),
            vm((3, n_m, ROWS + PAD, COLS), BF16),
            vm((3, n_m, ROWS + PAD, COLS), BF16),
            vm((n_m, ROWS, COLS), BF16),
            vm((COLS, COLS), F32),
            vm(coded, BF16),
            vm(coded, BF16),
            vm((n_m, 2 * COLS, ROWS), F32),
            dma((2, 2, 4)), dma((2, 2, 4)), dma((4,)), dma((2, 4)), dma,
            dma((2, n_m)), dma((2, n_m)), dma((2, n_m)), dma((n_m,)), dma,
            dma((3, n_m)), dma((3, n_m)),
            dma, dma, dma, dma, dma,
            dma, dma, dma, dma, dma, dma, dma,
        ],
        compiler_params=pltpu.CompilerParams(
            collective_id=0, has_side_effects=True, vmem_limit_bytes=60 * 2**20
        ),
        cost_estimate=pl.CostEstimate(flops=12 * 10**9, bytes_accessed=10**7, transcendentals=0),
    )(grad_out, hidden, down_weight)
    ig, wg = pl.pallas_call(
        place,
        out_shape=tuple(jax.ShapeDtypeStruct(a.shape, a.dtype) for a in (ig, wg)),
        in_specs=[pl.BlockSpec(memory_space=pltpu.VMEM)] * 2,
        out_specs=(pl.BlockSpec(memory_space=pl.ANY),) * 2,
        scratch_shapes=[dma((2,))],
    )(ig, wg)
    return ig, wg.reshape(1, n_m * COLS, 1, COLS)


def solution(mesh):
    placed = (P(("tok", "ffn"), "wid"), P(("tok", "wid"), "ffn"), P("ffn", "wid"))
    return jax.shard_map(
        shards,
        mesh=mesh,
        in_specs=placed,
        out_specs=(P(("tok", "wid"), "ffn"), P("tok", "ffn", "wid", None)),
        check_vma=False,
    )
```

```python
import functools

import jax
import jax.numpy as jnp
from jax import lax
from jax.experimental import pallas as pl
from jax.experimental.pallas import tpu as pltpu
from jax.sharding import PartitionSpec as P

F32, BF16 = jnp.float32, jnp.bfloat16
MESH = pl.DeviceIdType.MESH
COLS = 256
ROWS = 128
PAD = 16
STEP = 32
SPAN = 240.0
ARRIVE = (-3, 0, 1, 2)
LEAVE = (-3, 2, -1, 3)
NEAR = (-3, 4, -1, 5)
FIRST = 4
LAG = 6
LAST = 8


def encode(dst, value):
    n = value.shape[0]
    top = jnp.max(jnp.abs(value), axis=0, keepdims=True)
    scale = (1.0 / jnp.maximum(top, 1e-30)).astype(BF16).astype(F32)
    for b in blocks(n):
        u = value[b : b + STEP] * scale
        y = jnp.exp2(jnp.abs(u) * SPAN - SPAN / 2)
        dst[b : b + STEP, :] = jnp.where(u < 0.0, -y, y).astype(BF16)
    dst[n:, :] = jnp.broadcast_to(scale, (PAD, value.shape[1])).astype(BF16)


def decode(src, b):
    n = src.shape[0] - PAD
    scale = src[n:, :].astype(F32)[0:1]
    y = src[b : b + STEP, :].astype(F32)
    u = (jnp.log2(jnp.abs(y)) + SPAN / 2) * (1.0 / (SPAN * scale))
    return jnp.where(y < 0.0, -u, u)


def blocks(n):
    return range(0, n, STEP)


def straight(tr, j):
    return True


def kernel(
    g_in, h_in, w_in, ig_out, wg_out,
    G, GS, H, HT, W, WS, igp, igs, igr, igo, sums, wgs, wgr, wgo,
    gA, gBC, gZ4, gZ, gS, hA, hBC, hS, hZ, wS, iR, q, lW, lG, lH, lO, lP,
    sG, sGS, sH, sHS, sW, sI, sWG,
):
    n_m = H.shape[0]
    t, f, w = lax.axis_index("tok"), lax.axis_index("ffn"), lax.axis_index("wid")
    y, zh, x, c = f // 2, f % 2, w // 2, w % 2
    d = 1 - 2 * c
    half = t // 2
    mid = (t == 1) | (t == 2)
    end = jnp.logical_not(mid)
    xp, xs = lax.rem(x + d + 4, 4), lax.rem(x - d + 4, 4)
    yp, ys = lax.rem(y + d + 4, 4), lax.rem(y - d + 4, 4)
    x2, y2 = lax.rem(x + 2, 4), lax.rem(y + 2, 4)
    to_xp, to_xs, to_sib = {"wid": xp * 2 + c}, {"wid": xs * 2 + c}, {"wid": x * 2 + 1 - c}
    to_x2, to_y2 = {"wid": x2 * 2 + c}, {"ffn": y2 * 2 + zh}
    to_yp, to_ys, to_z4 = {"ffn": yp * 2 + zh}, {"ffn": ys * 2 + zh}, {"ffn": y * 2 + 1 - zh}
    near = t + 1 - 2 * (t % 2)
    to_zp, to_zq, to_zd = {"tok": near}, {"tok": 3 - t}, {"tok": near, "ffn": y * 2 + 1 - zh}

    def send(src, dst, ssem, rsem, dev):
        pltpu.make_async_remote_copy(
            src_ref=src, dst_ref=dst, send_sem=ssem, recv_sem=rsem, device_id=dev, device_id_type=MESH
        ).start()

    def local(src, dst, sem):
        pltpu.make_async_copy(src, dst, sem).start()

    def wait(ref, sem):
        pltpu.make_async_copy(ref, ref, sem).wait()

    def cols(i):
        return pl.ds(pl.multiple_of(i * COLS, COLS), COLS)

    def rows(i, n=ROWS):
        return pl.ds(pl.multiple_of(i * n, n), n)

    def in_cols(j):
        base = jnp.where(j < 2, 3 - j, j - 2)
        return cols(base + half * (3 - 2 * base))

    def gblk(tr, z, yy, j):
        return G.at[rows(tr * 8 + z * 4 + yy), cols(j)]

    def hblk(m, tr, xx):
        return H.at[m, rows(tr * 8 + c * 4 + xx)]

    def zsel(s):
        return zh if s == 0 else 1 - zh

    def to_ring_y(src, tr, s, j):
        dst = gblk(tr, zsel(s), y, j)
        if straight(tr, j):
            for dev in (to_yp, to_ys, to_y2):
                send(src, dst, sG, gBC.at[tr, s, j], dev)
        else:
            send(src, dst, sG, gA.at[tr, s, j], to_yp)
            send(src, dst, sG, gBC.at[tr, s, j], to_ys)

    def own_y(j):
        to_ring_y(gblk(0, zh, y, j), 0, 0, j)

    def to_ring_x(src, tr, m):
        dst = hblk(m, tr, x)
        if tr == 1:
            for dev in (to_xp, to_xs, to_x2):
                send(src, dst, sH, hBC.at[tr, m], dev)
        else:
            send(src, dst, sH, hA.at[tr, m], to_xp)
            send(src, dst, sH, hBC.at[tr, m], to_xs)

    def own_x(m):
        to_ring_x(hblk(m, 0, x), 0, m)

    def own_z(m):
        send(hblk(m, 0, x), hblk(m, 1, x), sH, hZ.at[m], to_zp)

    def own_z4(j):
        send(gblk(0, zh, y, j), gblk(0, zh, y, j), sG, gZ4.at[j], to_z4)

    def own_gz(j):
        send(gblk(0, zh, y, j), gblk(1, zh, y, j), sG, gZ.at[0, j], to_zp)

    for j in range(4):
        local(g_in.at[:, in_cols(j)], gblk(0, zh, y, j), lG)
        local(w_in.at[:, in_cols(j)], W.at[:, cols(j)], lW)
    for m in range(n_m):
        local(h_in.at[:, cols(m)], hblk(m, 0, x), lH)

    barrier = pltpu.get_barrier_semaphore()
    for dev in (to_xp, to_xs, to_x2, to_sib, to_yp, to_ys, to_y2, to_z4, to_zp, to_zd):
        pl.semaphore_signal(barrier, inc=1, device_id=dev, device_id_type=MESH)

    @pl.when(mid)
    def _():
        pl.semaphore_signal(barrier, inc=1, device_id=to_zq, device_id_type=MESH)
        pl.semaphore_wait(barrier, 11)

    @pl.when(end)
    def _():
        pl.semaphore_wait(barrier, 10)

    wait(G.at[0:ROWS], lG)
    wait(H.at[:, 0:ROWS], lH)

    @pl.when(end)
    def _():
        own_gz(0)
        own_z(0)
        send(gblk(0, zh, y, 0), gblk(1, zh, y, 0), sG, gZ.at[1, 0], to_zd)
        own_z(1)
        own_z(2)

    own_z4(0)
    own_x(0)
    own_y(0)
    own_x(1)
    own_x(2)
    own_x(3)
    own_x(4)

    blk = G.at[0:ROWS, 0:COLS]
    two = G.at[0 : 2 * ROWS, 0:COLS]
    three = G.at[0 : 3 * ROWS, 0:COLS]

    def spread_y(tr, s, j):
        to_ring_y(gblk(tr, zsel(s), y, j), tr, s, j)

    def full_y(tr, j):
        for s in range(2):
            wait(three if straight(tr, j) else two, gBC.at[tr, s, j])

    def pass_y(tr, s, j):
        z = zsel(s)
        wait(blk, gA.at[tr, s, j])
        send(gblk(tr, z, ys, j), gblk(tr, z, ys, j), sG, gBC.at[tr, s, j], to_yp)

    def near_x(m):
        wait(blk, hA.at[0, m])
        send(hblk(m, 0, xs), hblk(m, 0, xs), sH, hBC.at[0, m], to_xp)

    def spread_x(m):
        wait(blk, hZ.at[m])
        to_ring_x(hblk(m, 1, x), 1, m)

    def share(tr, m):
        wait(three if tr == 1 else two, hBC.at[tr, m])
        own = H.at[m, rows(2 * tr + c, 4 * ROWS)]
        send(own, own, sHS, hS.at[tr, m], to_sib)

    def share_g(j):
        full_y(0, j)
        send(G.at[rows(1 - c, 4 * ROWS), cols(j)], GS.at[:, cols(j)], sGS, gS, to_sib)

    near_x(0)

    @pl.when(end)
    def _():
        near_x(1)
        own_z(3)

    wait(blk, gZ4.at[0])
    spread_y(0, 1, 0)

    @pl.when(mid)
    def _():
        near_x(1)
        wait(blk, gZ.at[0, 0])
        spread_y(1, 0, 0)
        wait(blk, gZ.at[1, 0])
        spread_y(1, 1, 0)
        spread_x(0)

    own_z4(1)
    own_z4(2)
    own_z4(3)
    own_y(1)

    @pl.when(end)
    def _():
        own_z(4)

    @pl.when(mid)
    def _():
        spread_x(1)

    near_x(2)
    own_x(5)
    share(0, 0)

    @pl.when(mid)
    def _():
        share(1, 0)

    def step(s, _):
        def at(k):
            return pl.when(s == k)

        @pl.when(s < n_m - 6)
        def _():
            own_x(s + 6)

        @pl.when(s < n_m - 3)
        def _():
            near_x(s + 3)

        @pl.when(end & (s < n_m - 5))
        def _():
            own_z(s + 5)

        @pl.when(mid & (s < n_m - 2))
        def _():
            spread_x(s + 2)

        @pl.when(s < n_m - 1)
        def _():
            share(0, s + 1)

            @pl.when(mid)
            def _():
                share(1, s + 1)

        @at(0)
        def _():
            share_g(0)

            @pl.when(mid)
            def _():
                full_y(1, 0)

        @pl.when(s < n_m)
        def _():
            wait(H.at[0, 0 : 4 * ROWS], hS.at[0, s])

            @pl.when(mid)
            def _():
                wait(H.at[0, 0 : 4 * ROWS], hS.at[1, s])
                HT[s] = H[s].T
                encode(wgs.at[0, s], jnp.dot(HT[s], G[:, 0:COLS], preferred_element_type=F32))
                send(wgs.at[0, s], wgr.at[0, s], sWG, q.at[0, s], to_zq)

        for j, k in ((1, LAG), (3, LAST)):

            @pl.when(mid & (s == k))
            def _():
                full_y(1, j)

        @pl.when(mid & (s >= LAG) & (s < n_m + LAG))
        def _():
            m = s - LAG
            encode(wgs.at[1, m], jnp.dot(HT[m], G[:, COLS : 2 * COLS], preferred_element_type=F32))
            send(wgs.at[1, m], wgr.at[1, m], sWG, q.at[1, m], to_zq)

        for j in (1, 2, 3):

            @at(ARRIVE[j] + 2)
            def _():
                share_g(j)

            @at(ARRIVE[j])
            def _():
                wait(blk, gZ4.at[j])
                spread_y(0, 1, j)

                if j < 3:
                    own_y(j + 1)

        for j in (1, 3):

            @pl.when(end & (s == LEAVE[j]))
            def _():
                own_gz(j)
                send(gblk(0, 1 - zh, y, j), gblk(1, 1 - zh, y, j), sG, gZ.at[1, j], to_zp)

            @pl.when(mid & (s == NEAR[j]))
            def _():
                for k in range(2):
                    wait(blk, gZ.at[k, j])
                    spread_y(1, k, j)

        @at(0)
        def _():
            wait(W, lW)

        @pl.when(s < 4)
        def _():
            send(W.at[:, cols(s)], WS.at[:, cols(s)], sW, wS, to_sib)

        @at(FIRST)
        def _():
            wait(WS, wS)
            wait(GS, gS)

        for k in range(1):
            i = s - FIRST

            @pl.when((i >= 0) & (i < n_m))
            def _():
                nt = (((1,), (1,)), ((), ()))
                part = lax.dot_general(G[rows(c, 4 * ROWS), :], W[cols(i), :], nt, preferred_element_type=F32)
                part += lax.dot_general(GS[...], WS[cols(i), :], nt, preferred_element_type=F32)
                igp[i] = part.reshape(4, ROWS, COLS)
                encode(igs.at[0, i], igp[i, x2])
                send(igs.at[0, i], igr.at[0, i], sI, iR.at[0, i], to_xp)
                encode(igs.at[1, i], igp[i, xs])
                send(igs.at[1, i], igr.at[1, i], sI, iR.at[1, i], to_xs)

        for k in range(1):
            l = s - FIRST - 2

            @pl.when((l >= 0) & (l < n_m))
            def _():
                wait(igr.at[0, l], iR.at[0, l])
                for b in blocks(ROWS):
                    igp[l, xp, b : b + STEP] += decode(igr.at[0, l], b)
                encode(igs.at[2, l], igp[l, xp])
                send(igs.at[2, l], igr.at[2, l], sI, iR.at[2, l], to_xp)

        for k in range(1):
            n = s - FIRST - 4

            @pl.when((n >= 0) & (n < n_m))
            def _():
                wait(igr.at[1, n], iR.at[1, n])
                wait(igr.at[2, n], iR.at[2, n])
                for b in blocks(ROWS):
                    total = igp[n, x, b : b + STEP] + decode(igr.at[1, n], b) + decode(igr.at[2, n], b)
                    igo[n, b : b + STEP] = total.astype(BF16)
                local(igo.at[n], ig_out.at[:, cols(n)], lO)

        def store(u, part, src):
            for b in blocks(COLS):
                value = part[b : b + STEP] + decode(src, b)
                for l in range(2):
                    wgo[u, pl.ds(2 * b + l, STEP, stride=2), :] = value[:, l * ROWS : (l + 1) * ROWS]
            local(wgo.at[u], wg_out.at[rows(u, 2 * COLS)], lP)

        @pl.when(mid & (s >= 4) & (s < n_m + 4))
        def _():
            u = s - 4
            part = jnp.dot(HT[u, :, 0 : 8 * ROWS], G[0 : 8 * ROWS, 2 * COLS : 3 * COLS], preferred_element_type=F32)
            wait(wgr.at[0, u], q.at[0, u])
            for b in blocks(COLS):
                sums[b : b + STEP] = part[b : b + STEP] + decode(wgr.at[0, u], b)
            encode(wgs.at[2, u], sums[...])
            send(wgs.at[2, u], wgr.at[2, u], sWG, q.at[2, u], to_zp)

        @pl.when(mid & (s >= LAST) & (s < n_m + LAST))
        def _():
            u = s - LAST
            part = jnp.dot(HT[u], G[:, 3 * COLS :], preferred_element_type=F32)
            wait(wgr.at[1, u], q.at[1, u])
            store(u, part, wgr.at[1, u])

        @pl.when(end & (s >= 6) & (s < n_m + 6))
        def _():
            u = s - 6
            part = jnp.dot(H[u, 0 : 8 * ROWS].T, G[0 : 8 * ROWS, 2 * COLS : 3 * COLS], preferred_element_type=F32)
            wait(wgr.at[2, u], q.at[2, u])
            store(u, part, wgr.at[2, u])

        return 0

    lax.fori_loop(0, n_m + max(LAST, FIRST + 4), step, 0)

    @pl.when(mid)
    def _():
        wait(G.at[0 : 46 * ROWS // 4], sG)
        wait(H.at[:, 0 : 6 * ROWS], sH)
        wait(H.at[:, 0 : 8 * ROWS], sHS)
        wait(wgs, sWG)

    @pl.when(end)
    def _():
        wait(G.at[0 : 34 * ROWS // 4], sG)
        wait(H.at[:, 0 : 4 * ROWS], sH)
        wait(H.at[:, 0 : 4 * ROWS], sHS)

    wait(GS, sGS)
    wait(W, sW)
    wait(igs, sI)
    wait(igo, lO)
    wait(wgo, lP)


def place(ig, wg, ig_out, wg_out, ig_held, wg_held, sems):
    n = sems.shape[0] - 1
    size = wg.shape[0] // n
    moves = [(ig, ig_held, ig_out)]
    for i in range(n):
        part = pl.ds(i * size, size)
        moves.append((wg.at[part], wg_held.at[part], wg_out.at[part]))
    loads = [pltpu.make_async_copy(a, b, sems.at[i]) for i, (a, b, _) in enumerate(moves)]
    stores = [pltpu.make_async_copy(b, c, sems.at[i]) for i, (_, b, c) in enumerate(moves)]
    for load in loads:
        load.start()
    for load, store in zip(loads, stores):
        load.wait()
        store.start()
    for store in stores:
        store.wait()


def shards(grad_out, hidden, down_weight):
    n_m = hidden.shape[1] // COLS
    dma = pltpu.SemaphoreType.DMA
    vm = pltpu.VMEM
    coded = (3, n_m, COLS + PAD, COLS)
    ig, wg = pl.pallas_call(
        kernel,
        out_shape=(
            jax.ShapeDtypeStruct((ROWS, n_m * COLS), BF16),
            jax.ShapeDtypeStruct((n_m * COLS * 2, ROWS), F32),
        ),
        in_specs=[pl.BlockSpec(memory_space=pl.ANY)] * 3,
        out_specs=(pl.BlockSpec(memory_space=pl.ANY),) * 2,
        scratch_shapes=[
            vm((16 * ROWS, 4 * COLS), BF16),
            vm((4 * ROWS, 4 * COLS), BF16),
            vm((n_m, 16 * ROWS, COLS), BF16),
            vm((n_m, COLS, 16 * ROWS), BF16),
            vm((n_m * COLS, 4 * COLS), BF16),
            vm((n_m * COLS, 4 * COLS), BF16),
            vm((n_m, 4, ROWS, COLS), F32),
            vm((3, n_m, ROWS + PAD, COLS), BF16),
            vm((3, n_m, ROWS + PAD, COLS), BF16),
            vm((n_m, ROWS, COLS), BF16),
            vm((COLS, COLS), F32),
            vm(coded, BF16),
            vm(coded, BF16),
            vm((n_m, 2 * COLS, ROWS), F32),
            dma((2, 2, 4)), dma((2, 2, 4)), dma((4,)), dma((2, 4)), dma,
            dma((2, n_m)), dma((2, n_m)), dma((2, n_m)), dma((n_m,)), dma,
            dma((3, n_m)), dma((3, n_m)),
            dma, dma, dma, dma, dma,
            dma, dma, dma, dma, dma, dma, dma,
        ],
        compiler_params=pltpu.CompilerParams(
            collective_id=0, has_side_effects=True, vmem_limit_bytes=60 * 2**20
        ),
        cost_estimate=pl.CostEstimate(flops=12 * 10**9, bytes_accessed=10**7, transcendentals=0),
    )(grad_out, hidden, down_weight)
    ig, wg = pl.pallas_call(
        place,
        out_shape=tuple(jax.ShapeDtypeStruct(a.shape, a.dtype) for a in (ig, wg)),
        in_specs=[pl.BlockSpec(memory_space=pl.ANY)] * 2,
        out_specs=(pl.BlockSpec(memory_space=pl.ANY),) * 2,
        scratch_shapes=[vm(ig.shape, BF16), vm(wg.shape, F32), dma((8,))],
    )(ig, wg)
    return ig, wg.reshape(1, n_m * COLS, 1, COLS)


def solution(mesh):
    placed = (P(("tok", "ffn"), "wid"), P(("tok", "wid"), "ffn"), P("ffn", "wid"))
    return jax.shard_map(
        shards,
        mesh=mesh,
        in_specs=placed,
        out_specs=(P(("tok", "wid"), "ffn"), P("tok", "ffn", "wid", None)),
        check_vma=False,
    )
```

```python
import functools

import jax
import jax.numpy as jnp
from jax import lax
from jax.experimental import pallas as pl
from jax.experimental.pallas import tpu as pltpu
from jax.sharding import PartitionSpec as P

F32, BF16 = jnp.float32, jnp.bfloat16
MESH = pl.DeviceIdType.MESH
COLS = 256
ROWS = 128
PAD = 16
STEP = 32
SPAN = 240.0
ARRIVE = (-3, 0, 1, 2)
LEAVE = (-3, 2, -1, 3)
NEAR = (-3, 4, -1, 5)
FIRST = 4
LAG = 6
LAST = 8


def encode(dst, value):
    n = value.shape[0]
    top = jnp.max(jnp.abs(value), axis=0, keepdims=True)
    scale = (1.0 / jnp.maximum(top, 1e-30)).astype(BF16).astype(F32)
    for b in blocks(n):
        u = value[b : b + STEP] * scale
        y = jnp.exp2(jnp.abs(u) * SPAN - SPAN / 2)
        dst[b : b + STEP, :] = jnp.where(u < 0.0, -y, y).astype(BF16)
    dst[n:, :] = jnp.broadcast_to(scale, (PAD, value.shape[1])).astype(BF16)


def decode(src, b):
    n = src.shape[0] - PAD
    scale = src[n:, :].astype(F32)[0:1]
    y = src[b : b + STEP, :].astype(F32)
    u = (jnp.log2(jnp.abs(y)) + SPAN / 2) * (1.0 / (SPAN * scale))
    return jnp.where(y < 0.0, -u, u)


def blocks(n):
    return range(0, n, STEP)


def straight(tr, j):
    return True


def kernel(
    g_in, h_in, w_in, ig_out, wg_out,
    G, GS, H, HT, W, WS, igp, igs, igr, igo, sums, wgs, wgr, wgo,
    gA, gBC, gZ4, gZ, gS, hA, hBC, hS, hZ, wS, iR, q, lW, lG, lH, lO, lP,
    sG, sGS, sH, sHS, sW, sI, sWG,
):
    n_m = H.shape[0]
    t, f, w = lax.axis_index("tok"), lax.axis_index("ffn"), lax.axis_index("wid")
    y, zh, x, c = f // 2, f % 2, w // 2, w % 2
    d = 1 - 2 * c
    half = t // 2
    mid = (t == 1) | (t == 2)
    end = jnp.logical_not(mid)
    xp, xs = lax.rem(x + d + 4, 4), lax.rem(x - d + 4, 4)
    yp, ys = lax.rem(y + d + 4, 4), lax.rem(y - d + 4, 4)
    x2, y2 = lax.rem(x + 2, 4), lax.rem(y + 2, 4)
    to_xp, to_xs, to_sib = {"wid": xp * 2 + c}, {"wid": xs * 2 + c}, {"wid": x * 2 + 1 - c}
    to_x2, to_y2 = {"wid": x2 * 2 + c}, {"ffn": y2 * 2 + zh}
    to_yp, to_ys, to_z4 = {"ffn": yp * 2 + zh}, {"ffn": ys * 2 + zh}, {"ffn": y * 2 + 1 - zh}
    near = t + 1 - 2 * (t % 2)
    to_zp, to_zq, to_zd = {"tok": near}, {"tok": 3 - t}, {"tok": near, "ffn": y * 2 + 1 - zh}

    def send(src, dst, ssem, rsem, dev):
        pltpu.make_async_remote_copy(
            src_ref=src, dst_ref=dst, send_sem=ssem, recv_sem=rsem, device_id=dev, device_id_type=MESH
        ).start()

    def local(src, dst, sem):
        pltpu.make_async_copy(src, dst, sem).start()

    def wait(ref, sem):
        pltpu.make_async_copy(ref, ref, sem).wait()

    def cols(i):
        return pl.ds(pl.multiple_of(i * COLS, COLS), COLS)

    def rows(i, n=ROWS):
        return pl.ds(pl.multiple_of(i * n, n), n)

    def in_cols(j):
        base = jnp.where(j < 2, 3 - j, j - 2)
        return cols(base + half * (3 - 2 * base))

    def gblk(tr, z, yy, j):
        return G.at[rows(tr * 8 + z * 4 + yy), cols(j)]

    def hblk(m, tr, xx):
        return H.at[m, rows(tr * 8 + c * 4 + xx)]

    def zsel(s):
        return zh if s == 0 else 1 - zh

    def to_ring_y(src, tr, s, j):
        dst = gblk(tr, zsel(s), y, j)
        if straight(tr, j):
            for dev in (to_yp, to_ys, to_y2):
                send(src, dst, sG, gBC.at[tr, s, j], dev)
        else:
            send(src, dst, sG, gA.at[tr, s, j], to_yp)
            send(src, dst, sG, gBC.at[tr, s, j], to_ys)

    def own_y(j):
        to_ring_y(gblk(0, zh, y, j), 0, 0, j)

    def to_ring_x(src, tr, m):
        dst = hblk(m, tr, x)
        if tr == 1:
            for dev in (to_xp, to_xs, to_x2):
                send(src, dst, sH, hBC.at[tr, m], dev)
        else:
            send(src, dst, sH, hA.at[tr, m], to_xp)
            send(src, dst, sH, hBC.at[tr, m], to_xs)

    def own_x(m):
        to_ring_x(hblk(m, 0, x), 0, m)

    def own_z(m):
        send(hblk(m, 0, x), hblk(m, 1, x), sH, hZ.at[m], to_zp)

    def own_z4(j):
        send(gblk(0, zh, y, j), gblk(0, zh, y, j), sG, gZ4.at[j], to_z4)

    def own_gz(j):
        send(gblk(0, zh, y, j), gblk(1, zh, y, j), sG, gZ.at[0, j], to_zp)

    for j in range(4):
        local(g_in.at[:, in_cols(j)], gblk(0, zh, y, j), lG)
        local(w_in.at[:, in_cols(j)], W.at[:, cols(j)], lW)
    for m in range(n_m):
        local(h_in.at[:, cols(m)], hblk(m, 0, x), lH)

    barrier = pltpu.get_barrier_semaphore()
    for dev in (to_xp, to_xs, to_x2, to_sib, to_yp, to_ys, to_y2, to_z4, to_zp, to_zd):
        pl.semaphore_signal(barrier, inc=1, device_id=dev, device_id_type=MESH)

    @pl.when(mid)
    def _():
        pl.semaphore_signal(barrier, inc=1, device_id=to_zq, device_id_type=MESH)
        pl.semaphore_wait(barrier, 11)

    @pl.when(end)
    def _():
        pl.semaphore_wait(barrier, 10)

    wait(G.at[0:ROWS], lG)
    wait(H.at[:, 0:ROWS], lH)

    @pl.when(end)
    def _():
        own_gz(0)
        own_z(0)
        send(gblk(0, zh, y, 0), gblk(1, zh, y, 0), sG, gZ.at[1, 0], to_zd)
        own_z(1)
        own_z(2)

    own_z4(0)
    own_x(0)
    own_y(0)
    own_x(1)
    own_x(2)
    own_x(3)
    own_x(4)

    blk = G.at[0:ROWS, 0:COLS]
    two = G.at[0 : 2 * ROWS, 0:COLS]
    three = G.at[0 : 3 * ROWS, 0:COLS]

    def spread_y(tr, s, j):
        to_ring_y(gblk(tr, zsel(s), y, j), tr, s, j)

    def full_y(tr, j):
        for s in range(2):
            wait(three if straight(tr, j) else two, gBC.at[tr, s, j])

    def pass_y(tr, s, j):
        z = zsel(s)
        wait(blk, gA.at[tr, s, j])
        send(gblk(tr, z, ys, j), gblk(tr, z, ys, j), sG, gBC.at[tr, s, j], to_yp)

    def near_x(m):
        wait(blk, hA.at[0, m])
        send(hblk(m, 0, xs), hblk(m, 0, xs), sH, hBC.at[0, m], to_xp)

    def spread_x(m):
        wait(blk, hZ.at[m])
        to_ring_x(hblk(m, 1, x), 1, m)

    def share(tr, m):
        wait(three if tr == 1 else two, hBC.at[tr, m])
        own = H.at[m, rows(2 * tr + c, 4 * ROWS)]
        send(own, own, sHS, hS.at[tr, m], to_sib)

    def share_g(j):
        full_y(0, j)
        send(G.at[rows(1 - c, 4 * ROWS), cols(j)], GS.at[:, cols(j)], sGS, gS, to_sib)

    near_x(0)

    @pl.when(end)
    def _():
        near_x(1)
        own_z(3)

    wait(blk, gZ4.at[0])
    spread_y(0, 1, 0)

    @pl.when(mid)
    def _():
        near_x(1)
        wait(blk, gZ.at[0, 0])
        spread_y(1, 0, 0)
        wait(blk, gZ.at[1, 0])
        spread_y(1, 1, 0)
        spread_x(0)

    own_z4(1)
    own_z4(2)
    own_z4(3)
    own_y(1)

    @pl.when(end)
    def _():
        own_z(4)

    @pl.when(mid)
    def _():
        spread_x(1)

    near_x(2)
    own_x(5)
    share(0, 0)

    @pl.when(mid)
    def _():
        share(1, 0)

    def step(s, _):
        def at(k):
            return pl.when(s == k)

        @pl.when(s < n_m - 6)
        def _():
            own_x(s + 6)

        @pl.when(s < n_m - 3)
        def _():
            near_x(s + 3)

        @pl.when(end & (s < n_m - 5))
        def _():
            own_z(s + 5)

        @at(0)
        def _():
            share_g(0)

            @pl.when(mid)
            def _():
                full_y(1, 0)

        @pl.when(s < n_m)
        def _():
            wait(H.at[0, 0 : 4 * ROWS], hS.at[0, s])

            @pl.when(mid)
            def _():
                wait(H.at[0, 0 : 4 * ROWS], hS.at[1, s])
                HT[s] = H[s].T
                encode(wgs.at[0, s], jnp.dot(HT[s], G[:, 0:COLS], preferred_element_type=F32))
                send(wgs.at[0, s], wgr.at[0, s], sWG, q.at[0, s], to_zq)

        @pl.when(mid & (s < n_m - 2))
        def _():
            spread_x(s + 2)

        @pl.when(s < n_m - 1)
        def _():
            share(0, s + 1)

            @pl.when(mid)
            def _():
                share(1, s + 1)

        for j, k in ((1, LAG), (3, LAST)):

            @pl.when(mid & (s == k))
            def _():
                full_y(1, j)

        @pl.when(mid & (s >= LAG) & (s < n_m + LAG))
        def _():
            m = s - LAG
            encode(wgs.at[1, m], jnp.dot(HT[m], G[:, COLS : 2 * COLS], preferred_element_type=F32))
            send(wgs.at[1, m], wgr.at[1, m], sWG, q.at[1, m], to_zq)

        for j in (1, 2, 3):

            @at(ARRIVE[j] + 2)
            def _():
                share_g(j)

            @at(ARRIVE[j])
            def _():
                wait(blk, gZ4.at[j])
                spread_y(0, 1, j)

                if j < 3:
                    own_y(j + 1)

        for j in (1, 3):

            @pl.when(end & (s == LEAVE[j]))
            def _():
                own_gz(j)
                send(gblk(0, 1 - zh, y, j), gblk(1, 1 - zh, y, j), sG, gZ.at[1, j], to_zp)

            @pl.when(mid & (s == NEAR[j]))
            def _():
                for k in range(2):
                    wait(blk, gZ.at[k, j])
                    spread_y(1, k, j)

        @at(0)
        def _():
            wait(W, lW)

        @pl.when(s < 4)
        def _():
            send(W.at[:, cols(s)], WS.at[:, cols(s)], sW, wS, to_sib)

        @at(FIRST)
        def _():
            wait(WS, wS)
            wait(GS, gS)

        for k in range(1):
            i = s - FIRST

            @pl.when((i >= 0) & (i < n_m))
            def _():
                nt = (((1,), (1,)), ((), ()))
                part = lax.dot_general(G[rows(c, 4 * ROWS), :], W[cols(i), :], nt, preferred_element_type=F32)
                part += lax.dot_general(GS[...], WS[cols(i), :], nt, preferred_element_type=F32)
                igp[i] = part.reshape(4, ROWS, COLS)
                encode(igs.at[0, i], igp[i, x2])
                send(igs.at[0, i], igr.at[0, i], sI, iR.at[0, i], to_xp)
                encode(igs.at[1, i], igp[i, xs])
                send(igs.at[1, i], igr.at[1, i], sI, iR.at[1, i], to_xs)

        for k in range(1):
            l = s - FIRST - 2

            @pl.when((l >= 0) & (l < n_m))
            def _():
                wait(igr.at[0, l], iR.at[0, l])
                for b in blocks(ROWS):
                    igp[l, xp, b : b + STEP] += decode(igr.at[0, l], b)
                encode(igs.at[2, l], igp[l, xp])
                send(igs.at[2, l], igr.at[2, l], sI, iR.at[2, l], to_xp)

        for k in range(1):
            n = s - FIRST - 4

            @pl.when((n >= 0) & (n < n_m))
            def _():
                wait(igr.at[1, n], iR.at[1, n])
                wait(igr.at[2, n], iR.at[2, n])
                for b in blocks(ROWS):
                    total = igp[n, x, b : b + STEP] + decode(igr.at[1, n], b) + decode(igr.at[2, n], b)
                    igo[n, b : b + STEP] = total.astype(BF16)
                local(igo.at[n], ig_out.at[:, cols(n)], lO)

        def store(u, part, src):
            for b in blocks(COLS):
                value = part[b : b + STEP] + decode(src, b)
                for l in range(2):
                    wgo[u, pl.ds(2 * b + l, STEP, stride=2), :] = value[:, l * ROWS : (l + 1) * ROWS]
            local(wgo.at[u], wg_out.at[rows(u, 2 * COLS)], lP)

        @pl.when(mid & (s >= 4) & (s < n_m + 4))
        def _():
            u = s - 4
            part = jnp.dot(HT[u, :, 0 : 8 * ROWS], G[0 : 8 * ROWS, 2 * COLS : 3 * COLS], preferred_element_type=F32)
            wait(wgr.at[0, u], q.at[0, u])
            for b in blocks(COLS):
                sums[b : b + STEP] = part[b : b + STEP] + decode(wgr.at[0, u], b)
            encode(wgs.at[2, u], sums[...])
            send(wgs.at[2, u], wgr.at[2, u], sWG, q.at[2, u], to_zp)

        @pl.when(mid & (s >= LAST) & (s < n_m + LAST))
        def _():
            u = s - LAST
            part = jnp.dot(HT[u], G[:, 3 * COLS :], preferred_element_type=F32)
            wait(wgr.at[1, u], q.at[1, u])
            store(u, part, wgr.at[1, u])

        @pl.when(end & (s >= 6) & (s < n_m + 6))
        def _():
            u = s - 6
            part = jnp.dot(H[u, 0 : 8 * ROWS].T, G[0 : 8 * ROWS, 2 * COLS : 3 * COLS], preferred_element_type=F32)
            wait(wgr.at[2, u], q.at[2, u])
            store(u, part, wgr.at[2, u])

        return 0

    lax.fori_loop(0, n_m + max(LAST, FIRST + 4), step, 0)

    @pl.when(mid)
    def _():
        wait(G.at[0 : 46 * ROWS // 4], sG)
        wait(H.at[:, 0 : 6 * ROWS], sH)
        wait(H.at[:, 0 : 8 * ROWS], sHS)
        wait(wgs, sWG)

    @pl.when(end)
    def _():
        wait(G.at[0 : 34 * ROWS // 4], sG)
        wait(H.at[:, 0 : 4 * ROWS], sH)
        wait(H.at[:, 0 : 4 * ROWS], sHS)

    wait(GS, sGS)
    wait(W, sW)
    wait(igs, sI)
    wait(igo, lO)
    wait(wgo, lP)


def place(ig, wg, ig_out, wg_out, ig_held, wg_held, sems):
    n = sems.shape[0] - 1
    size = wg.shape[0] // n
    moves = [(ig, ig_held, ig_out)]
    for i in range(n):
        part = pl.ds(i * size, size)
        moves.append((wg.at[part], wg_held.at[part], wg_out.at[part]))
    loads = [pltpu.make_async_copy(a, b, sems.at[i]) for i, (a, b, _) in enumerate(moves)]
    stores = [pltpu.make_async_copy(b, c, sems.at[i]) for i, (_, b, c) in enumerate(moves)]
    for load in loads:
        load.start()
    for load, store in zip(loads, stores):
        load.wait()
        store.start()
    for store in stores:
        store.wait()


def shards(grad_out, hidden, down_weight):
    n_m = hidden.shape[1] // COLS
    dma = pltpu.SemaphoreType.DMA
    vm = pltpu.VMEM
    coded = (3, n_m, COLS + PAD, COLS)
    ig, wg = pl.pallas_call(
        kernel,
        out_shape=(
            jax.ShapeDtypeStruct((ROWS, n_m * COLS), BF16),
            jax.ShapeDtypeStruct((n_m * COLS * 2, ROWS), F32),
        ),
        in_specs=[pl.BlockSpec(memory_space=pl.ANY)] * 3,
        out_specs=(pl.BlockSpec(memory_space=pl.ANY),) * 2,
        scratch_shapes=[
            vm((16 * ROWS, 4 * COLS), BF16),
            vm((4 * ROWS, 4 * COLS), BF16),
            vm((n_m, 16 * ROWS, COLS), BF16),
            vm((n_m, COLS, 16 * ROWS), BF16),
            vm((n_m * COLS, 4 * COLS), BF16),
            vm((n_m * COLS, 4 * COLS), BF16),
            vm((n_m, 4, ROWS, COLS), F32),
            vm((3, n_m, ROWS + PAD, COLS), BF16),
            vm((3, n_m, ROWS + PAD, COLS), BF16),
            vm((n_m, ROWS, COLS), BF16),
            vm((COLS, COLS), F32),
            vm(coded, BF16),
            vm(coded, BF16),
            vm((n_m, 2 * COLS, ROWS), F32),
            dma((2, 2, 4)), dma((2, 2, 4)), dma((4,)), dma((2, 4)), dma,
            dma((2, n_m)), dma((2, n_m)), dma((2, n_m)), dma((n_m,)), dma,
            dma((3, n_m)), dma((3, n_m)),
            dma, dma, dma, dma, dma,
            dma, dma, dma, dma, dma, dma, dma,
        ],
        compiler_params=pltpu.CompilerParams(
            collective_id=0, has_side_effects=True, vmem_limit_bytes=60 * 2**20
        ),
        cost_estimate=pl.CostEstimate(flops=12 * 10**9, bytes_accessed=10**7, transcendentals=0),
    )(grad_out, hidden, down_weight)
    ig, wg = pl.pallas_call(
        place,
        out_shape=tuple(jax.ShapeDtypeStruct(a.shape, a.dtype) for a in (ig, wg)),
        in_specs=[pl.BlockSpec(memory_space=pl.ANY)] * 2,
        out_specs=(pl.BlockSpec(memory_space=pl.ANY),) * 2,
        scratch_shapes=[vm(ig.shape, BF16), vm(wg.shape, F32), dma((8,))],
    )(ig, wg)
    return ig, wg.reshape(1, n_m * COLS, 1, COLS)


def solution(mesh):
    placed = (P(("tok", "ffn"), "wid"), P(("tok", "wid"), "ffn"), P("ffn", "wid"))
    return jax.shard_map(
        shards,
        mesh=mesh,
        in_specs=placed,
        out_specs=(P(("tok", "wid"), "ffn"), P("tok", "ffn", "wid", None)),
        check_vma=False,
    )
```

```python
import functools

import jax
import jax.numpy as jnp
from jax import lax
from jax.experimental import pallas as pl
from jax.experimental.pallas import tpu as pltpu
from jax.sharding import PartitionSpec as P

F32, BF16 = jnp.float32, jnp.bfloat16
MESH = pl.DeviceIdType.MESH
COLS = 256
ROWS = 128
PAD = 16
STEP = 32
SPAN = 240.0
ARRIVE = (-3, 0, 1, 2)
LEAVE = (-3, 2, -1, 3)
NEAR = (-3, 4, -1, 5)
FIRST = 4
LAG = 6
LAST = 8


def encode(dst, value):
    n = value.shape[0]
    top = jnp.max(jnp.abs(value), axis=0, keepdims=True)
    scale = (1.0 / jnp.maximum(top, 1e-30)).astype(BF16).astype(F32)
    for b in blocks(n):
        u = value[b : b + STEP] * scale
        y = jnp.exp2(jnp.abs(u) * SPAN - SPAN / 2)
        dst[b : b + STEP, :] = jnp.where(u < 0.0, -y, y).astype(BF16)
    dst[n:, :] = jnp.broadcast_to(scale, (PAD, value.shape[1])).astype(BF16)


def decode(src, b):
    n = src.shape[0] - PAD
    scale = src[n:, :].astype(F32)[0:1]
    y = src[b : b + STEP, :].astype(F32)
    u = (jnp.log2(jnp.abs(y)) + SPAN / 2) * (1.0 / (SPAN * scale))
    return jnp.where(y < 0.0, -u, u)


def blocks(n):
    return range(0, n, STEP)


def straight(tr, j):
    return True


def kernel(
    g_in, h_in, w_in, ig_out, wg_out,
    G, GS, H, HT, W, WS, igp, igs, igr, igo, sums, wgs, wgr, wgo,
    gA, gBC, gZ4, gZ, gS, hA, hBC, hS, hZ, wS, iR, q, lW, lG, lH, lO, lP,
    sG, sGS, sH, sHS, sW, sI, sWG,
):
    n_m = H.shape[0]
    t, f, w = lax.axis_index("tok"), lax.axis_index("ffn"), lax.axis_index("wid")
    y, zh, x, c = f // 2, f % 2, w // 2, w % 2
    d = 1 - 2 * c
    half = t // 2
    mid = (t == 1) | (t == 2)
    end = jnp.logical_not(mid)
    xp, xs = lax.rem(x + d + 4, 4), lax.rem(x - d + 4, 4)
    yp, ys = lax.rem(y + d + 4, 4), lax.rem(y - d + 4, 4)
    x2, y2 = lax.rem(x + 2, 4), lax.rem(y + 2, 4)
    to_xp, to_xs, to_sib = {"wid": xp * 2 + c}, {"wid": xs * 2 + c}, {"wid": x * 2 + 1 - c}
    to_x2, to_y2 = {"wid": x2 * 2 + c}, {"ffn": y2 * 2 + zh}
    to_yp, to_ys, to_z4 = {"ffn": yp * 2 + zh}, {"ffn": ys * 2 + zh}, {"ffn": y * 2 + 1 - zh}
    near = t + 1 - 2 * (t % 2)
    to_zp, to_zq, to_zd = {"tok": near}, {"tok": 3 - t}, {"tok": near, "ffn": y * 2 + 1 - zh}

    def send(src, dst, ssem, rsem, dev):
        pltpu.make_async_remote_copy(
            src_ref=src, dst_ref=dst, send_sem=ssem, recv_sem=rsem, device_id=dev, device_id_type=MESH
        ).start()

    def local(src, dst, sem):
        pltpu.make_async_copy(src, dst, sem).start()

    def wait(ref, sem):
        pltpu.make_async_copy(ref, ref, sem).wait()

    def cols(i):
        return pl.ds(pl.multiple_of(i * COLS, COLS), COLS)

    def rows(i, n=ROWS):
        return pl.ds(pl.multiple_of(i * n, n), n)

    def in_cols(j):
        base = jnp.where(j < 2, 3 - j, j - 2)
        return cols(base + half * (3 - 2 * base))

    def gblk(tr, z, yy, j):
        return G.at[rows(tr * 8 + z * 4 + yy), cols(j)]

    def hblk(m, tr, xx):
        return H.at[m, rows(tr * 8 + c * 4 + xx)]

    def zsel(s):
        return zh if s == 0 else 1 - zh

    def to_ring_y(src, tr, s, j):
        dst = gblk(tr, zsel(s), y, j)
        if straight(tr, j):
            for dev in (to_yp, to_ys, to_y2):
                send(src, dst, sG, gBC.at[tr, s, j], dev)
        else:
            send(src, dst, sG, gA.at[tr, s, j], to_yp)
            send(src, dst, sG, gBC.at[tr, s, j], to_ys)

    def own_y(j):
        to_ring_y(gblk(0, zh, y, j), 0, 0, j)

    def to_ring_x(src, tr, m):
        dst = hblk(m, tr, x)
        if tr == 1:
            for dev in (to_xp, to_xs, to_x2):
                send(src, dst, sH, hBC.at[tr, m], dev)
        else:
            send(src, dst, sH, hA.at[tr, m], to_xp)
            send(src, dst, sH, hBC.at[tr, m], to_xs)

    def own_x(m):
        to_ring_x(hblk(m, 0, x), 0, m)

    def own_z(m):
        send(hblk(m, 0, x), hblk(m, 1, x), sH, hZ.at[m], to_zp)

    def own_z4(j):
        send(gblk(0, zh, y, j), gblk(0, zh, y, j), sG, gZ4.at[j], to_z4)

    def own_gz(j):
        send(gblk(0, zh, y, j), gblk(1, zh, y, j), sG, gZ.at[0, j], to_zp)

    for j in range(4):
        local(g_in.at[:, in_cols(j)], gblk(0, zh, y, j), lG)
        local(w_in.at[:, in_cols(j)], W.at[:, cols(j)], lW)
    for m in range(n_m):
        local(h_in.at[:, cols(m)], hblk(m, 0, x), lH)

    barrier = pltpu.get_barrier_semaphore()
    for dev in (to_xp, to_xs, to_x2, to_sib, to_yp, to_ys, to_y2, to_z4, to_zp, to_zd):
        pl.semaphore_signal(barrier, inc=1, device_id=dev, device_id_type=MESH)

    @pl.when(mid)
    def _():
        pl.semaphore_signal(barrier, inc=1, device_id=to_zq, device_id_type=MESH)
        pl.semaphore_wait(barrier, 11)

    @pl.when(end)
    def _():
        pl.semaphore_wait(barrier, 10)

    wait(G.at[0:ROWS], lG)
    wait(H.at[:, 0:ROWS], lH)

    @pl.when(end)
    def _():
        own_gz(0)
        own_z(0)
        send(gblk(0, zh, y, 0), gblk(1, zh, y, 0), sG, gZ.at[1, 0], to_zd)
        own_z(1)
        own_z(2)

    own_z4(0)
    own_x(0)
    own_y(0)
    own_x(1)
    own_x(2)
    own_x(3)
    own_x(4)

    blk = G.at[0:ROWS, 0:COLS]
    two = G.at[0 : 2 * ROWS, 0:COLS]
    three = G.at[0 : 3 * ROWS, 0:COLS]

    def spread_y(tr, s, j):
        to_ring_y(gblk(tr, zsel(s), y, j), tr, s, j)

    def full_y(tr, j):
        for s in range(2):
            wait(three if straight(tr, j) else two, gBC.at[tr, s, j])

    def pass_y(tr, s, j):
        z = zsel(s)
        wait(blk, gA.at[tr, s, j])
        send(gblk(tr, z, ys, j), gblk(tr, z, ys, j), sG, gBC.at[tr, s, j], to_yp)

    def near_x(m):
        wait(blk, hA.at[0, m])
        send(hblk(m, 0, xs), hblk(m, 0, xs), sH, hBC.at[0, m], to_xp)

    def spread_x(m):
        wait(blk, hZ.at[m])
        to_ring_x(hblk(m, 1, x), 1, m)

    def share(tr, m):
        wait(three if tr == 1 else two, hBC.at[tr, m])
        own = H.at[m, rows(2 * tr + c, 4 * ROWS)]
        send(own, own, sHS, hS.at[tr, m], to_sib)

    def share_g(j):
        full_y(0, j)
        send(G.at[rows(1 - c, 4 * ROWS), cols(j)], GS.at[:, cols(j)], sGS, gS, to_sib)

    near_x(0)

    @pl.when(end)
    def _():
        near_x(1)
        own_z(3)

    wait(blk, gZ4.at[0])
    spread_y(0, 1, 0)

    @pl.when(mid)
    def _():
        near_x(1)
        wait(blk, gZ.at[0, 0])
        spread_y(1, 0, 0)
        wait(blk, gZ.at[1, 0])
        spread_y(1, 1, 0)
        spread_x(0)

    own_z4(1)
    own_z4(2)
    own_z4(3)
    own_y(1)

    @pl.when(end)
    def _():
        own_z(4)

    @pl.when(mid)
    def _():
        spread_x(1)

    near_x(2)
    own_x(5)
    share(0, 0)

    @pl.when(mid)
    def _():
        share(1, 0)

    def step(s, _):
        def at(k):
            return pl.when(s == k)

        @pl.when(s < n_m - 6)
        def _():
            own_x(s + 6)

        @pl.when(s < n_m - 3)
        def _():
            near_x(s + 3)

        @pl.when(end & (s < n_m - 5))
        def _():
            own_z(s + 5)

        @at(0)
        def _():
            share_g(0)

            @pl.when(mid)
            def _():
                full_y(1, 0)

        @pl.when(s < n_m)
        def _():
            wait(H.at[0, 0 : 4 * ROWS], hS.at[0, s])

            @pl.when(mid)
            def _():
                wait(H.at[0, 0 : 4 * ROWS], hS.at[1, s])
                HT[s] = H[s].T
                encode(wgs.at[0, s], jnp.dot(HT[s], G[:, 0:COLS], preferred_element_type=F32))
                send(wgs.at[0, s], wgr.at[0, s], sWG, q.at[0, s], to_zq)

        @pl.when(mid & (s < n_m - 2))
        def _():
            spread_x(s + 2)

        @pl.when(s < n_m - 1)
        def _():
            share(0, s + 1)

            @pl.when(mid)
            def _():
                share(1, s + 1)

        for j, k in ((1, LAG), (3, LAST)):

            @pl.when(mid & (s == k))
            def _():
                full_y(1, j)

        @pl.when(mid & (s >= LAG) & (s < n_m + LAG))
        def _():
            m = s - LAG
            encode(wgs.at[1, m], jnp.dot(HT[m], G[:, COLS : 2 * COLS], preferred_element_type=F32))
            send(wgs.at[1, m], wgr.at[1, m], sWG, q.at[1, m], to_zq)

        for j in (1, 2, 3):

            @at(ARRIVE[j] + 2)
            def _():
                share_g(j)

            @at(ARRIVE[j])
            def _():
                wait(blk, gZ4.at[j])
                spread_y(0, 1, j)

                if j < 3:
                    own_y(j + 1)

        for j in (1, 3):

            @pl.when(end & (s == LEAVE[j]))
            def _():
                own_gz(j)
                send(gblk(0, 1 - zh, y, j), gblk(1, 1 - zh, y, j), sG, gZ.at[1, j], to_zp)

            @pl.when(mid & (s == NEAR[j]))
            def _():
                for k in range(2):
                    wait(blk, gZ.at[k, j])
                    spread_y(1, k, j)

        @at(0)
        def _():
            wait(W, lW)

        @pl.when(s < 4)
        def _():
            send(W.at[:, cols(s)], WS.at[:, cols(s)], sW, wS, to_sib)

        @at(FIRST)
        def _():
            wait(WS, wS)
            wait(GS, gS)

        for k in range(1):
            i = s - FIRST

            @pl.when((i >= 0) & (i < n_m))
            def _():
                nt = (((1,), (1,)), ((), ()))
                part = lax.dot_general(G[rows(c, 4 * ROWS), :], W[cols(i), :], nt, preferred_element_type=F32)
                part += lax.dot_general(GS[...], WS[cols(i), :], nt, preferred_element_type=F32)
                igp[i] = part.reshape(4, ROWS, COLS)
                encode(igs.at[0, i], igp[i, x2])
                send(igs.at[0, i], igr.at[0, i], sI, iR.at[0, i], to_xp)
                encode(igs.at[1, i], igp[i, xs])
                send(igs.at[1, i], igr.at[1, i], sI, iR.at[1, i], to_xs)

        for k in range(1):
            l = s - FIRST - 2

            @pl.when((l >= 0) & (l < n_m))
            def _():
                wait(igr.at[0, l], iR.at[0, l])
                for b in blocks(ROWS):
                    igp[l, xp, b : b + STEP] += decode(igr.at[0, l], b)
                encode(igs.at[2, l], igp[l, xp])
                send(igs.at[2, l], igr.at[2, l], sI, iR.at[2, l], to_xp)

        for k in range(1):
            n = s - FIRST - 4

            @pl.when((n >= 0) & (n < n_m))
            def _():
                wait(igr.at[1, n], iR.at[1, n])
                wait(igr.at[2, n], iR.at[2, n])
                for b in blocks(ROWS):
                    total = igp[n, x, b : b + STEP] + decode(igr.at[1, n], b) + decode(igr.at[2, n], b)
                    igo[n, b : b + STEP] = total.astype(BF16)
                local(igo.at[n], ig_out.at[:, cols(n)], lO)

        def store(u, part, src):
            for b in blocks(COLS):
                value = part[b : b + STEP] + decode(src, b)
                for l in range(2):
                    wgo[u, pl.ds(2 * b + l, STEP, stride=2), :] = value[:, l * ROWS : (l + 1) * ROWS]
            local(wgo.at[u, 0 : 2 * COLS], wg_out.at[rows(u, 2 * COLS)], lP)

        @pl.when(mid & (s >= 4) & (s < n_m + 4))
        def _():
            u = s - 4
            part = jnp.dot(HT[u, :, 0 : 8 * ROWS], G[0 : 8 * ROWS, 2 * COLS : 3 * COLS], preferred_element_type=F32)
            wait(wgr.at[0, u], q.at[0, u])
            for b in blocks(COLS):
                sums[b : b + STEP] = part[b : b + STEP] + decode(wgr.at[0, u], b)
            encode(wgs.at[2, u], sums[...])
            send(wgs.at[2, u], wgr.at[2, u], sWG, q.at[2, u], to_zp)

        @pl.when(mid & (s >= LAST) & (s < n_m + LAST))
        def _():
            u = s - LAST
            part = jnp.dot(HT[u], G[:, 3 * COLS :], preferred_element_type=F32)
            wait(wgr.at[1, u], q.at[1, u])
            store(u, part, wgr.at[1, u])

        @pl.when(end & (s >= 6) & (s < n_m + 6))
        def _():
            u = s - 6
            part = jnp.dot(H[u, 0 : 8 * ROWS].T, G[0 : 8 * ROWS, 2 * COLS : 3 * COLS], preferred_element_type=F32)
            wait(wgr.at[2, u], q.at[2, u])
            store(u, part, wgr.at[2, u])

        return 0

    lax.fori_loop(0, n_m + max(LAST, FIRST + 4), step, 0)

    @pl.when(mid)
    def _():
        wait(G.at[0 : 46 * ROWS // 4], sG)
        wait(H.at[:, 0 : 6 * ROWS], sH)
        wait(H.at[:, 0 : 8 * ROWS], sHS)
        wait(wgs, sWG)

    @pl.when(end)
    def _():
        wait(G.at[0 : 34 * ROWS // 4], sG)
        wait(H.at[:, 0 : 4 * ROWS], sH)
        wait(H.at[:, 0 : 4 * ROWS], sHS)

    wait(GS, sGS)
    wait(W, sW)
    wait(igs, sI)
    wait(igo, lO)
    wait(wgo.at[:, 0 : 2 * COLS], lP)


def place(ig, wg, ig_out, wg_out, ig_held, wg_held, sems):
    n = sems.shape[0] - 1
    size = wg.shape[0] // n
    moves = [(ig, ig_held, ig_out)]
    for i in range(n):
        part = pl.ds(i * size, size)
        moves.append((wg.at[part], wg_held.at[part], wg_out.at[part]))
    loads = [pltpu.make_async_copy(a, b, sems.at[i]) for i, (a, b, _) in enumerate(moves)]
    stores = [pltpu.make_async_copy(b, c, sems.at[i]) for i, (_, b, c) in enumerate(moves)]
    for load in loads:
        load.start()
    for load, store in zip(loads, stores):
        load.wait()
        store.start()
    for store in stores:
        store.wait()


def shards(grad_out, hidden, down_weight):
    n_m = hidden.shape[1] // COLS
    dma = pltpu.SemaphoreType.DMA
    vm = pltpu.VMEM
    coded = (3, n_m, COLS + PAD, COLS)
    ig, wg = pl.pallas_call(
        kernel,
        out_shape=(
            jax.ShapeDtypeStruct((ROWS, n_m * COLS), BF16),
            jax.ShapeDtypeStruct((n_m * COLS * 2, ROWS), F32),
        ),
        in_specs=[pl.BlockSpec(memory_space=pl.ANY)] * 3,
        out_specs=(pl.BlockSpec(memory_space=pl.ANY),) * 2,
        scratch_shapes=[
            vm((16 * ROWS, 4 * COLS), BF16),
            vm((4 * ROWS, 4 * COLS), BF16),
            vm((n_m, 16 * ROWS, COLS), BF16),
            vm((n_m, COLS, 16 * ROWS), BF16),
            vm((n_m * COLS, 4 * COLS), BF16),
            vm((n_m * COLS, 4 * COLS), BF16),
            vm((n_m, 4, ROWS, COLS), F32),
            vm((3, n_m, ROWS + PAD, COLS), BF16),
            vm((3, n_m, ROWS + PAD, COLS), BF16),
            vm((n_m, ROWS, COLS), BF16),
            vm((COLS, COLS), F32),
            vm(coded, BF16),
            vm(coded, BF16),
            vm((n_m, 2 * COLS + 8, ROWS), F32),
            dma((2, 2, 4)), dma((2, 2, 4)), dma((4,)), dma((2, 4)), dma,
            dma((2, n_m)), dma((2, n_m)), dma((2, n_m)), dma((n_m,)), dma,
            dma((3, n_m)), dma((3, n_m)),
            dma, dma, dma, dma, dma,
            dma, dma, dma, dma, dma, dma, dma,
        ],
        compiler_params=pltpu.CompilerParams(
            collective_id=0, has_side_effects=True, vmem_limit_bytes=60 * 2**20
        ),
        cost_estimate=pl.CostEstimate(flops=12 * 10**9, bytes_accessed=10**7, transcendentals=0),
    )(grad_out, hidden, down_weight)
    ig, wg = pl.pallas_call(
        place,
        out_shape=tuple(jax.ShapeDtypeStruct(a.shape, a.dtype) for a in (ig, wg)),
        in_specs=[pl.BlockSpec(memory_space=pl.ANY)] * 2,
        out_specs=(pl.BlockSpec(memory_space=pl.ANY),) * 2,
        scratch_shapes=[vm(ig.shape, BF16), vm(wg.shape, F32), dma((8,))],
    )(ig, wg)
    return ig, wg.reshape(1, n_m * COLS, 1, COLS)


def solution(mesh):
    placed = (P(("tok", "ffn"), "wid"), P(("tok", "wid"), "ffn"), P("ffn", "wid"))
    return jax.shard_map(
        shards,
        mesh=mesh,
        in_specs=placed,
        out_specs=(P(("tok", "wid"), "ffn"), P("tok", "ffn", "wid", None)),
        check_vma=False,
    )
```
